32 devices in a mesh: dom: 8 (over y, x, core), blk: 4 (over z).
Axes of the slice: x: 2, y: 2, z: 4, core: 2. Of those that a mesh axis runs over, the one named last changes fastest.
Arguments:
- node_features: bfloat16 [8192, 512], P(('dom', 'blk')), may hold values from -6 to 6
- norm_gain: float32 [512], replicated, may hold values from 0.25 to 1.75
- w_query: bfloat16 [512, 512], replicated, may hold values from -0.25 to 0.25
- w_key: bfloat16 [512, 512], replicated, may hold values from -0.25 to 0.25
- w_value: bfloat16 [512, 512], replicated, may hold values from -0.25 to 0.25
- w_out: bfloat16 [512, 512], replicated, may hold values from -1.5 to 1.5
- w_message: bfloat16 [512, 512], replicated, may hold values from -1 to 1
- node_cluster: int32 [8192], P(('dom', 'blk')), may hold values from 0 to 15
- block_pattern: int32 [32, 4], P(('dom', 'blk')), may hold values from 0 to 1, as said below
- send_rows: int32 [256, 128], P(('dom', 'blk')), may hold values from 0 to 255
- send_counts: int32 [256], P(('dom', 'blk')), may hold values from 32 to 128, as said below
- edge_src: int32 [131072], P(('dom', 'blk')), may hold values from 0 to 1023
- edge_dst: int32 [131072], P(('dom', 'blk')), may hold values from 0 to 255
- out_grad: bfloat16 [8192, 512], P(('dom', 'blk')), may hold values from -6 to 6
Outputs:
- layer_out: bfloat16 [8192, 512], P(('dom', 'blk'))
- feature_grad: bfloat16 [8192, 512], P(('dom', 'blk'))
- weight_grads: float32 [5, 512, 512], replicated
- gain_grad: float32 [512], replicated
The draws below stay inside these ranges and needn't reach their ends.
Inputs may be any that keep to these rules, and one draw needn't show every extreme that they name: `block_pattern`: row g has a 1 at column (g mod 4); other entries are 0 or 1. `send_counts`: entry g * 8 + p is how many leading slots of device g's block to dom peer p are live; every device has one peer whose block has all 128 slots live.
All inputs are finite; a program needn't handle non-finite values.
Results may differ from the reference program's by a relative error of at most 0.013.
Values may be sent and summed in bfloat16 or wider, within the bound.
A program may use at most 128 MiB of HBM per device.

```python
import math
import jax
import jax.numpy as jnp
import numpy as np
from jax import lax

D = 512
HEADS = 8
HEAD_DIM = 64
ROWS = 256
CLUSTERS = 16
CAP = 128
EDGES = 4096
NODES = 8192
N_DOM = 8
N_BLK = 4


def draw_block_pattern(key, part):
    random_bits = jax.random.randint(key, (N_DOM * N_BLK, N_BLK), 0, 2)
    own_column = (jnp.arange(N_DOM * N_BLK) % N_BLK)[:, None] == jnp.arange(N_BLK)[None, :]
    return jnp.where(own_column, 1, random_bits).astype(jnp.int32)


def draw_send_counts(key, part):
    first_key, second_key = jax.random.split(key)
    drawn = jax.random.randint(first_key, (N_DOM * N_BLK, N_DOM), CAP // 4, CAP + 1)
    full_peer = jax.random.randint(second_key, (N_DOM * N_BLK, 1), 0, N_DOM)
    drawn = jnp.where(jnp.arange(N_DOM)[None, :] == full_peer, CAP, drawn)
    return drawn.reshape(-1).astype(jnp.int32)


def set_ends(result, key, least, high):
    longest = result.shape.index(max(result.shape))
    spots = []
    for shift in (0, 1):
        where = [jax.random.randint(jax.random.fold_in(key, axis), (), 0, length) for axis, length in enumerate(result.shape)]
        where[longest] = (where[longest] + shift) % result.shape[longest]
        spots.append(tuple(where))
    return result.at[spots[0]].set(least).at[spots[1]].set(high)


def block_levels(stream_key, dims, cuts, low, largest):
    def one(dim, shards_of):
        draws = jax.random.uniform(jax.random.fold_in(jax.random.fold_in(stream_key, 6), dim), (shards_of,), jnp.float32, low / len(cuts), largest / len(cuts))
        return jnp.repeat(jnp.exp(draws), dims[dim] // shards_of).reshape((-1,) + (1,) * (len(dims) - dim - 1))

    level = one(*cuts[0])
    for cut in cuts[1:]:
        level = level * one(*cut)
    return level


def rank_bounds(number_of, lean):
    portions = [(1 << 20) // math.isqrt(standing ** lean) + 1 for standing in range(1, number_of + 1)]
    width = 1 + sum(portions) // (1 << 30)
    return np.cumsum(np.array([max(1, weight // width) for weight in portions]))


def ranked(rng, dims, number_of, slope):
    grid = rank_bounds(number_of, slope)
    pick = jax.random.randint(jax.random.fold_in(rng, 1), dims, 0, int(grid[number_of - 1]))
    grade = jnp.searchsorted(jnp.asarray(grid, jnp.int32), pick, side="right")
    return jax.random.permutation(jax.random.fold_in(rng, 2), number_of)[grade].astype(jnp.int32)


def gaussian(own_key, dims, width, bound, shards=(), held_as=jnp.bfloat16):
    level = block_levels(own_key, dims, shards, -0.22, 0.18) if shards else 1.0
    result = jax.random.normal(own_key, dims, jnp.float32) * width * level
    return jnp.minimum(jnp.maximum(result, -bound), bound).astype(held_as)


def setup_inputs(seed: int = 0) -> dict:
    streams_of = jax.random.split(jax.random.key(seed), 15)
    return {
        "node_features": gaussian(streams_of[0], (NODES, D), 1.0, 6.0, ((0, 32),)),
        "norm_gain": jnp.clip(1.0 + 0.15 * jax.random.normal(streams_of[1], (D,), jnp.float32), 0.25, 1.75),
        "w_query": gaussian(streams_of[2], (D, D), D ** -0.5, 0.25),
        "w_key": gaussian(streams_of[3], (D, D), D ** -0.5, 0.25),
        "w_value": gaussian(streams_of[4], (D, D), D ** -0.5, 0.25),
        "w_out": gaussian(streams_of[5], (D, D), (D // 32) ** -0.5, 1.5),
        "w_message": gaussian(streams_of[6], (D, D), (D // 16) ** -0.5, 1.0),
        "node_cluster": set_ends(jax.random.randint(streams_of[7], (NODES,), 0, CLUSTERS), jax.random.fold_in(streams_of[7], 1), 0, CLUSTERS - 1).astype(jnp.int32),
        "block_pattern": draw_block_pattern(jax.random.fold_in(streams_of[14], 71), 0),
        "send_rows": set_ends(jax.random.randint(streams_of[9], (N_DOM * N_BLK * N_DOM, CAP), 0, ROWS), jax.random.fold_in(streams_of[9], 1), 0, ROWS - 1).astype(jnp.int32),
        "send_counts": draw_send_counts(jax.random.fold_in(streams_of[14], 71), 0),
        "edge_src": set_ends(jax.random.randint(streams_of[11], (N_DOM * N_BLK * EDGES,), 0, N_DOM * CAP), jax.random.fold_in(streams_of[11], 1), 0, (N_DOM * CAP) - 1).astype(jnp.int32),
        "edge_dst": set_ends(ranked(streams_of[12], (N_DOM * N_BLK * EDGES,), ROWS, 2), jax.random.fold_in(streams_of[12], 3), 0, ROWS - 1).astype(jnp.int32),
        "out_grad": gaussian(streams_of[13], (NODES, D), 1.0, 6.0, ((0, 32),)),
    }


epsilon = 1e-06
score_shift = 8.0

def rounded(array):
    return lax.optimization_barrier(array.astype(jnp.bfloat16))

def rms_norm(features, norm_gain):
    scaling = lax.rsqrt(lax.optimization_barrier(jnp.mean(features * features, axis=-1, keepdims=True)) + epsilon)
    return features * scaling * norm_gain

def head_norm(projected):
    head_view = projected.reshape(projected.shape[0], HEADS, HEAD_DIM)
    scaling = lax.rsqrt(lax.optimization_barrier(jnp.mean(head_view * head_view, axis=-1, keepdims=True)) + epsilon)
    return (head_view * scaling).reshape(projected.shape)

def masked_weights(query_heads, query_labels, key_heads, key_labels, pattern_row):
    owners = jnp.arange(N_BLK * ROWS, dtype=jnp.int32) // ROWS
    block_flags = pattern_row[owners]
    allowed = (query_labels[:, None] == key_labels[None, :]) & (block_flags[None, :] == 1)
    scaling = score_shift / HEAD_DIM
    scores = jnp.einsum('rhe,khe->hrk', query_heads.astype(jnp.float32), key_heads.astype(jnp.float32)) * scaling
    return jnp.where(allowed[None], jnp.exp(scores - score_shift), 0.0)

def group_forward(group):
    query_all, key_all, value_all, label_all, pattern = group

    def one_device(position):
        query_part = lax.dynamic_slice_in_dim(query_all, position * ROWS, ROWS, 0)
        label_part = lax.dynamic_slice_in_dim(label_all, position * ROWS, ROWS, 0)
        weights = masked_weights(query_part, label_part, key_all, label_all, pattern[position])
        denom = lax.optimization_barrier(jnp.sum(weights, axis=2)).T
        numer = jnp.einsum('hrk,khe->rhe', rounded(weights).astype(jnp.float32), value_all.astype(jnp.float32))
        return (numer, denom)
    return lax.map(one_device, jnp.arange(N_BLK, dtype=jnp.int32))

def group_backward(group):
    query_all, key_all, value_all, grad_all, correction_all, label_all, pattern = group
    scaling = score_shift / HEAD_DIM

    def one_device(running, position):
        key_total, value_total = running
        query_part = lax.dynamic_slice_in_dim(query_all, position * ROWS, ROWS, 0)
        grad_part = lax.dynamic_slice_in_dim(grad_all, position * ROWS, ROWS, 0)
        correction_part = lax.dynamic_slice_in_dim(correction_all, position * ROWS, ROWS, 0)
        label_part = lax.dynamic_slice_in_dim(label_all, position * ROWS, ROWS, 0)
        weights = masked_weights(query_part, label_part, key_all, label_all, pattern[position])
        grad_dots = jnp.einsum('rhe,khe->hrk', grad_part.astype(jnp.float32), value_all.astype(jnp.float32))
        slopes = rounded(weights * (grad_dots - correction_part.T[:, :, None])).astype(jnp.float32)
        slope_blocks = slopes.reshape(HEADS, ROWS, N_BLK, ROWS)
        key_blocks = key_all.astype(jnp.float32).reshape(N_BLK, ROWS, HEADS, HEAD_DIM)
        dq_blocks = jnp.einsum('hrbk,bkhe->brhe', slope_blocks, key_blocks) * scaling
        dq_part = lax.optimization_barrier(jnp.sum(rounded(dq_blocks).astype(jnp.float32), axis=0))
        dk_part = jnp.einsum('hrk,rhe->khe', slopes, query_part.astype(jnp.float32)) * scaling
        dv_part = jnp.einsum('hrk,rhe->khe', rounded(weights).astype(jnp.float32), grad_part.astype(jnp.float32))
        key_total = key_total + rounded(dk_part).astype(jnp.float32)
        value_total = value_total + rounded(dv_part).astype(jnp.float32)
        return ((key_total, value_total), dq_part)
    zero_block = jnp.zeros((N_BLK * ROWS, HEADS, HEAD_DIM), jnp.float32)
    (key_total, value_total), dq_parts = lax.scan(one_device, (zero_block, zero_block), jnp.arange(N_BLK, dtype=jnp.int32))
    return (dq_parts.reshape(N_BLK * ROWS, HEADS, HEAD_DIM), key_total, value_total)

def reference(node_features, norm_gain, w_query, w_key, w_value, w_out, w_message, node_cluster, block_pattern, send_rows, send_counts, edge_src, edge_dst, out_grad):
    features = node_features.astype(jnp.float32)
    normed_f, norm_pull = jax.vjp(rms_norm, features, norm_gain)
    normed = rounded(normed_f)
    node_blocks = normed.reshape(N_DOM, N_BLK, ROWS, D)
    row_table = send_rows.reshape(N_DOM, N_BLK, N_DOM, CAP)
    live_table = jnp.arange(CAP, dtype=jnp.int32)[None, None, None, :] < send_counts.reshape(N_DOM, N_BLK, N_DOM)[..., None]
    source_table = edge_src.reshape(N_DOM, N_BLK, EDGES)
    target_table = edge_dst.reshape(N_DOM, N_BLK, EDGES)

    def count_edges(targets):
        return jax.ops.segment_sum(jnp.ones(targets.shape, jnp.float32), targets, ROWS)
    degree = jnp.maximum(jax.vmap(jax.vmap(count_edges))(target_table), 1.0)

    def pick_rows(node_rows, chosen):
        return node_rows[chosen]

    def receive(target):
        chosen = row_table[:, :, target]
        live_now = live_table[:, :, target]
        sent = jax.vmap(jax.vmap(pick_rows))(node_blocks, chosen)
        sent = jnp.where(live_now[..., None], sent, jnp.zeros((), sent.dtype))
        slot_table = jnp.transpose(sent, (1, 0, 2, 3)).reshape(N_BLK, N_DOM * CAP, D)

        def average(table_rows, sources, targets, counts):
            picked = table_rows[sources].astype(jnp.float32)
            return rounded(jax.ops.segment_sum(picked, targets, ROWS) / counts[:, None])
        return jax.vmap(average)(slot_table, source_table[target], target_table[target], degree[target])
    mean_rows = lax.map(receive, jnp.arange(N_DOM, dtype=jnp.int32)).reshape(NODES, D)
    local_term = jnp.dot(mean_rows, w_message, preferred_element_type=jnp.float32)
    query_f, query_pull = jax.vjp(head_norm, jnp.dot(normed, w_query, preferred_element_type=jnp.float32))
    key_f, key_pull = jax.vjp(head_norm, jnp.dot(normed, w_key, preferred_element_type=jnp.float32))
    queries = rounded(query_f)
    keys = rounded(key_f)
    values = rounded(jnp.dot(normed, w_value, preferred_element_type=jnp.float32))

    def grouped(array):
        return array.reshape(N_DOM, N_BLK * ROWS, HEADS, HEAD_DIM)
    labels = node_cluster.reshape(N_DOM, N_BLK * ROWS)
    pattern = block_pattern.reshape(N_DOM, N_BLK, N_BLK)
    numer, denom = lax.map(group_forward, (grouped(queries), grouped(keys), grouped(values), labels, pattern))
    numer = numer.reshape(NODES, HEADS, HEAD_DIM)
    denom = denom.reshape(NODES, HEADS)
    attn_heads = rounded(numer / denom[..., None])
    attn_rows = attn_heads.reshape(NODES, D)
    attn_proj = jnp.dot(attn_rows, w_out, preferred_element_type=jnp.float32)
    layer_out = (features + local_term + attn_proj).astype(jnp.bfloat16)
    grad_attn = jnp.dot(out_grad, w_out.T, preferred_element_type=jnp.float32).reshape(NODES, HEADS, HEAD_DIM)
    grad_heads = rounded(grad_attn / denom[..., None])
    correction = lax.optimization_barrier(jnp.sum(grad_attn * attn_heads.astype(jnp.float32), axis=-1)) / denom
    dq_heads, dk_heads, dv_heads = lax.map(group_backward, (grouped(queries), grouped(keys), grouped(values), grouped(grad_heads), correction.reshape(N_DOM, N_BLK * ROWS, HEADS), labels, pattern))
    dquery = rounded(query_pull(dq_heads.reshape(NODES, D))[0])
    dkey = rounded(key_pull(dk_heads.reshape(NODES, D))[0])
    dvalue = rounded(dv_heads.reshape(NODES, D))
    dmessage = rounded(jnp.dot(out_grad, w_message.T, preferred_element_type=jnp.float32) / degree.reshape(NODES)[:, None])
    message_blocks = dmessage.reshape(N_DOM, N_BLK, ROWS, D)

    def give_back(running, target):

        def per_device(message_rows, sources, targets):
            return rounded(jax.ops.segment_sum(message_rows[targets].astype(jnp.float32), sources, N_DOM * CAP)).astype(jnp.float32)
        slot_grads = jax.vmap(per_device)(message_blocks[target], source_table[target], target_table[target])
        returned = jnp.transpose(slot_grads.reshape(N_BLK, N_DOM, CAP, D), (1, 0, 2, 3))
        returned = jnp.where(live_table[:, :, target][..., None], returned, 0.0)

        def scatter_rows(grad_rows, chosen):
            return jax.ops.segment_sum(grad_rows, chosen, ROWS)
        return (running + jax.vmap(jax.vmap(scatter_rows))(returned, row_table[:, :, target]), None)
    halo_grad, unused = lax.scan(give_back, jnp.zeros((N_DOM, N_BLK, ROWS, D), jnp.float32), jnp.arange(N_DOM, dtype=jnp.int32))
    dnormed = jnp.dot(dquery, w_query.T, preferred_element_type=jnp.float32)
    dnormed = dnormed + jnp.dot(dkey, w_key.T, preferred_element_type=jnp.float32)
    dnormed = dnormed + jnp.dot(dvalue, w_value.T, preferred_element_type=jnp.float32)
    dnormed = dnormed + halo_grad.reshape(NODES, D)
    dfeatures, gain_grad = norm_pull(dnormed)
    feature_grad = (out_grad.astype(jnp.float32) + dfeatures).astype(jnp.bfloat16)
    weight_grads = jnp.stack([jnp.dot(normed.T, dquery, preferred_element_type=jnp.float32), jnp.dot(normed.T, dkey, preferred_element_type=jnp.float32), jnp.dot(normed.T, dvalue, preferred_element_type=jnp.float32), jnp.dot(attn_rows.T, out_grad, preferred_element_type=jnp.float32), jnp.dot(mean_rows.T, out_grad, preferred_element_type=jnp.float32)])
    return (layer_out, feature_grad, weight_grads, gain_grad)
```

```python
from functools import partial

import jax
import jax.numpy as jnp
from jax import lax
from jax.experimental import pallas as pl
from jax.experimental.pallas import tpu as pltpu
from jax.sharding import PartitionSpec as P

HEADS = 8
HEAD_DIM = 64
SCALE = 8.0 / HEAD_DIM
SHIFT = 8.0
EPS = 1e-06
MASKED = -1e30
EDGE_PART = 512
MESH = pl.DeviceIdType.MESH
F32 = jnp.float32
BF16 = jnp.bfloat16


def params(collective_id=None):
    return pltpu.CompilerParams(
        vmem_limit_bytes=56 * 1024 * 1024,
        collective_id=collective_id,
        has_side_effects=collective_id is not None,
    )


def mul(a, b, ca, cb):
    return lax.dot_general(a, b, (((ca,), (cb,)), ((), ())), preferred_element_type=F32)


def row_scale(x):
    return lax.rsqrt(jnp.mean(x * x, axis=-1, keepdims=True) + EPS)


def head_norm(x):
    view = x.reshape(HEADS, HEAD_DIM, x.shape[1])
    scaling = lax.rsqrt(jnp.mean(view * view, axis=1, keepdims=True) + EPS)
    return view * scaling, scaling


def head_norm_pull(y, scaling, dy):
    dy = dy.reshape(y.shape)
    dx = scaling * (dy - y * jnp.mean(y * dy, axis=1, keepdims=True))
    return dx.reshape(-1, y.shape[2])


def remote(src, dst, send, recv, axis, peer):
    return pltpu.make_async_remote_copy(
        src_ref=src, dst_ref=dst, send_sem=send, recv_sem=recv,
        device_id={axis: peer}, device_id_type=MESH,
    )


def exchange_kernel(
    nd, nb,
    feat, gout, gain, wm, meta, sidx, esrc, edst,
    feats, gouts, metas, mean_out, halo_out,
    sbuf, rbuf, sback, rback, cnt, onehot,
    own_sem, zsend, zrecv, asend, arecv, bsend, brecv,
):
    me = lax.axis_index("blk")
    my_dom = lax.axis_index("dom")
    rows = feat.shape[0]
    cap = sidx.shape[1]
    barrier = pltpu.get_barrier_semaphore()
    for k in range(1, nd):
        pl.semaphore_signal(
            barrier, inc=1, device_id={"dom": lax.rem(my_dom + k, nd)}, device_id_type=MESH
        )
    for k in range(1, nb):
        pl.semaphore_signal(
            barrier, inc=1, device_id={"blk": lax.rem(me + k, nb)}, device_id_type=MESH
        )
    pl.semaphore_wait(barrier, nd - 1 + nb - 1)

    own = ((feat, feats), (gout, gouts), (meta, metas))
    local = [pltpu.make_async_copy(s, d.at[me], own_sem.at[k]) for k, (s, d) in enumerate(own)]
    for c in local:
        c.start()

    def line_copy(step, way, k, block):
        src, dst = own[k]
        if step > 0:
            src = dst.at[block]
        peer = me + 1 if way == 0 else me - 1
        return remote(
            src, dst.at[block], zsend.at[way, step, k], zrecv.at[way, step, k], "blk", peer
        )

    def line_send(step, start):
        for way in range(2):
            sends = (me + 1 < nb) & (me - step >= 0) if way == 0 else (me >= 1) & (me + step < nb)
            block = me - step if way == 0 else me + step

            @pl.when(sends)
            def _():
                for k in range(3):
                    c = line_copy(step, way, k, block)
                    if start:
                        c.start()
                    else:
                        c.wait_send()

    def line_recv(step):
        for way in range(2):
            block = me - 1 - step if way == 0 else me + 1 + step
            got = block >= 0 if way == 0 else block < nb

            @pl.when(got)
            def _():
                for k in range(3):
                    line_copy(step, way, k, block).wait_recv()

    line_send(0, True)

    x = feat[...].astype(F32)
    normed = (x * row_scale(x) * gain[...]).astype(BF16)
    row_ids = lax.broadcasted_iota(jnp.int32, (rows, cap), 0)

    def swap(src, dst, send, recv, k, incoming):
        to = lax.rem(my_dom + k, nd)
        origin = lax.rem(my_dom + nd - k, nd)
        return remote(
            src.at[to], dst.at[origin if incoming else my_dom], send.at[k], recv.at[k], "dom", to
        )

    for p in range(nd):
        hot = jnp.where(row_ids == sidx[p : p + 1, :], 1.0, 0.0).astype(BF16)
        onehot[:, p * cap : (p + 1) * cap] = hot
        sbuf[p] = mul(hot, normed, 0, 0).astype(BF16)
    for k in range(1, nd):
        swap(sbuf, rbuf, asend, arecv, k, False).start()
    rbuf[my_dom] = sbuf[my_dom]

    slot_ids = lax.broadcasted_iota(jnp.int32, (nd * cap, EDGE_PART), 0)
    dst_ids = lax.broadcasted_iota(jnp.int32, (rows, EDGE_PART), 0)
    cnt[...] = jnp.zeros_like(cnt)

    def count(c, carry):
        hot_src = jnp.where(slot_ids == esrc[pl.ds(c, 1), :], 1.0, 0.0).astype(BF16)
        hot_dst = jnp.where(dst_ids == edst[pl.ds(c, 1), :], 1.0, 0.0).astype(BF16)
        cnt[...] += mul(hot_dst, hot_src, 1, 1)
        return carry

    lax.fori_loop(0, esrc.shape[0], count, 0)
    counts = cnt[...]
    degree = jnp.maximum(jnp.sum(counts, axis=1, keepdims=True), 1.0)
    counts = counts.astype(BF16)
    dmessage = (mul(gout[...], wm[...], 1, 1) / degree).astype(BF16)
    for p in range(nd):
        sback[p] = mul(counts[:, p * cap : (p + 1) * cap], dmessage, 0, 0).astype(BF16)
    for k in range(1, nd):
        swap(sback, rback, bsend, brecv, k, False).start()
    rback[my_dom] = sback[my_dom]

    if nb > 2:
        line_recv(0)
        line_send(1, True)
    for k in range(1, nd):
        swap(sbuf, rbuf, asend, arecv, k, True).wait_recv()
    table = rbuf[...].reshape(nd * cap, -1)
    mean_out[...] = (mul(counts, table, 1, 0) / degree).astype(BF16)
    for step in range(2, nb - 1):
        line_recv(step - 1)
        line_send(step, True)
    for k in range(1, nd):
        swap(sback, rback, bsend, brecv, k, True).wait_recv()
    back = rback[...].reshape(nd * cap, -1)
    halo_out[...] = mul(onehot[...], back, 1, 0)
    line_recv(nb - 2)
    for step in range(nb - 1):
        line_send(step, False)
    for k in range(1, nd):
        swap(sbuf, rbuf, asend, arecv, k, False).wait_send()
        swap(sback, rback, bsend, brecv, k, False).wait_send()
    for c in local:
        c.wait()


def exchange(nd, nb, feat, gout, gain, wm, meta, sidx, esrc, edst):
    rows, width = feat.shape
    cap = sidx.shape[1]
    vmem = pl.BlockSpec(memory_space=pltpu.VMEM)
    anywhere = pl.BlockSpec(memory_space=pl.ANY)
    slots = pltpu.VMEM((nd, cap, width), BF16)
    dma = pltpu.SemaphoreType.DMA
    return pl.pallas_call(
        partial(exchange_kernel, nd, nb),
        out_shape=[
            jax.ShapeDtypeStruct((nb, rows, width), BF16),
            jax.ShapeDtypeStruct((nb, rows, width), BF16),
            jax.ShapeDtypeStruct((nb, 8, rows), jnp.int32),
            jax.ShapeDtypeStruct((rows, width), BF16),
            jax.ShapeDtypeStruct((rows, width), F32),
        ],
        in_specs=[vmem] * 8,
        out_specs=[anywhere] * 3 + [vmem] * 2,
        scratch_shapes=[
            slots, slots, slots, slots,
            pltpu.VMEM((rows, nd * cap), F32),
            pltpu.VMEM((rows, nd * cap), BF16),
            dma((3,)),
            dma((2, nb, 3)), dma((2, nb, 3)),
            dma((nd,)), dma((nd,)), dma((nd,)), dma((nd,)),
        ],
        compiler_params=params(0),
    )(feat, gout, gain, wm, meta, sidx, esrc, edst)


def attend_kernel(
    feats, feat, gout, gain, wq, wk, wv, wo, mean, wm, key_labels, own_labels,
    layer, normed_all, attn_t, dq_t, stats,
    k_t, v_t, q_t, ga_t, bias, dq_f,
):
    x = feats[...].astype(F32)
    normed_all[...] = (x * row_scale(x) * gain[...]).astype(BF16)
    x = feat[...].astype(F32)
    normed = (x * row_scale(x) * gain[...]).astype(BF16)
    keys, _ = head_norm(mul(wk[...], normed_all[...], 0, 1))
    k_t[...] = keys.reshape(k_t.shape).astype(BF16)
    v_t[...] = mul(wv[...], normed_all[...], 0, 1).astype(BF16)
    queries, q_scaling = head_norm(mul(wq[...], normed, 0, 1))
    q_t[...] = (queries * SCALE).reshape(q_t.shape).astype(BF16)
    ga_t[...] = mul(wo[...], gout[...], 1, 1)
    bias[...] = jnp.where(key_labels[...] == own_labels[...], -SHIFT, MASKED)
    for h in range(HEADS):
        part = slice(h * HEAD_DIM, (h + 1) * HEAD_DIM)
        kh, vh, qh, ga = k_t[part, :], v_t[part, :], q_t[part, :], ga_t[part, :]
        weights = jnp.exp(mul(kh, qh, 0, 0) + bias[...])
        inv = 1.0 / jnp.sum(weights, axis=0, keepdims=True)
        attn = (mul(vh, weights.astype(BF16), 1, 0) * inv).astype(BF16)
        attn_t[part, :] = attn
        correction = jnp.sum(ga * attn.astype(F32), axis=0, keepdims=True) * inv
        stats[h : h + 1, :] = inv
        stats[HEADS + h : HEADS + h + 1, :] = correction
        dots = mul(vh, (ga * inv).astype(BF16), 0, 0)
        slopes = (weights * (dots - correction)).astype(BF16)
        dq_f[part, :] = mul(kh, slopes, 1, 0) * SCALE
    dq_t[...] = head_norm_pull(queries, q_scaling, dq_f[...]).astype(BF16)
    out = x + mul(mean[...], wm[...], 1, 0) + mul(attn_t[...], wo[...], 0, 0)
    layer[...] = out.astype(BF16)


def attend(feats, feat, gout, gain, wq, wk, wv, wo, mean, wm, key_labels, own_labels):
    rows, width = feat.shape
    total = feats.shape[0]
    vmem = pl.BlockSpec(memory_space=pltpu.VMEM)
    return pl.pallas_call(
        attend_kernel,
        out_shape=[
            jax.ShapeDtypeStruct((rows, width), BF16),
            jax.ShapeDtypeStruct((total, width), BF16),
            jax.ShapeDtypeStruct((width, rows), BF16),
            jax.ShapeDtypeStruct((width, rows), BF16),
            jax.ShapeDtypeStruct((2 * HEADS, rows), F32),
        ],
        in_specs=[vmem] * 12,
        out_specs=[vmem] * 5,
        scratch_shapes=[
            pltpu.VMEM((width, total), BF16),
            pltpu.VMEM((width, total), BF16),
            pltpu.VMEM((width, rows), BF16),
            pltpu.VMEM((width, rows), F32),
            pltpu.VMEM((total, rows), F32),
            pltpu.VMEM((width, rows), F32),
        ],
        compiler_params=params(),
    )(feats, feat, gout, gain, wq, wk, wv, wo, mean, wm, key_labels, own_labels)


def share_kernel(nb, x, out, own_sem, send, recv):
    me = lax.axis_index("blk")
    barrier = pltpu.get_barrier_semaphore()
    for k in range(1, nb):
        pl.semaphore_signal(
            barrier, inc=1, device_id={"blk": lax.rem(me + k, nb)}, device_id_type=MESH
        )
    pl.semaphore_wait(barrier, nb - 1)
    for k in range(1, nb):
        to = lax.rem(me + k, nb)
        remote(x, out.at[me], send.at[k], recv.at[k], "blk", to).start()
    out[me] = x[...]
    for k in range(1, nb):
        to = lax.rem(me + k, nb)
        origin = lax.rem(me + nb - k, nb)
        remote(x, out.at[origin], send.at[k], recv.at[k], "blk", to).wait()


def share(nb, x):
    vmem = pl.BlockSpec(memory_space=pltpu.VMEM)
    dma = pltpu.SemaphoreType.DMA
    return pl.pallas_call(
        partial(share_kernel, nb),
        out_shape=jax.ShapeDtypeStruct((nb,) + x.shape, x.dtype),
        in_specs=[vmem],
        out_specs=vmem,
        scratch_shapes=[dma((1,)), dma((nb,)), dma((nb,))],
        compiler_params=params(1),
    )(x)


def gradient_kernel(
    nb,
    normed_all, gouts, stats, feat, gout, gain, wq, wk, wv, wo,
    own_labels, query_labels, attn_t, dq_t, mean, halo,
    fgrad, wgrads, gain_out,
    q_t, gh_t, v_t, k_t, bias, dk_f, dv_f,
):
    width = wq.shape[0]
    half = width // 2
    x = feat[...].astype(F32)
    scaling = row_scale(x)
    xs = x * scaling
    normed = (xs * gain[...]).astype(BF16)
    queries, _ = head_norm(mul(wq[...], normed_all[...], 0, 1))
    q_t[...] = (queries * SCALE).reshape(q_t.shape).astype(BF16)
    inv = jnp.concatenate([stats[b, :HEADS, :] for b in range(nb)], axis=1)
    correction = jnp.concatenate([stats[b, HEADS:, :] for b in range(nb)], axis=1)
    ga = mul(wo[...], gouts[...], 1, 1).reshape(HEADS, HEAD_DIM, -1)
    gh_t[...] = (ga * inv[:, None, :]).reshape(gh_t.shape).astype(BF16)
    keys, k_scaling = head_norm(mul(wk[...], normed, 0, 1))
    k_t[...] = keys.reshape(k_t.shape).astype(BF16)
    v_t[...] = mul(wv[...], normed, 0, 1).astype(BF16)
    bias[...] = jnp.where(own_labels[...] == query_labels[...], -SHIFT, MASKED)
    for h in range(HEADS):
        part = slice(h * HEAD_DIM, (h + 1) * HEAD_DIM)
        kh, vh, qh, gh = k_t[part, :], v_t[part, :], q_t[part, :], gh_t[part, :]
        weights = jnp.exp(mul(kh, qh, 0, 0) + bias[...])
        dots = mul(vh, gh, 0, 0)
        slopes = (weights * (dots - correction[h : h + 1, :])).astype(BF16)
        dk_f[part, :] = mul(qh, slopes, 1, 1)
        dv_f[part, :] = mul(gh, weights.astype(BF16), 1, 1)
    dk_t = head_norm_pull(keys, k_scaling, dk_f[...]).astype(BF16)
    dv_t = dv_f[...].astype(BF16)
    dq = dq_t[...]
    dnormed = (mul(wq[...], dq, 1, 0) + mul(wk[...], dk_t, 1, 0) + mul(wv[...], dv_t, 1, 0)).T
    dnormed = dnormed + halo[...]
    dscaled = dnormed * gain[...]
    gain_out[...] = jnp.broadcast_to(
        jnp.sum(dnormed * xs, axis=0, keepdims=True), gain_out.shape
    )
    dx = scaling * (dscaled - xs * jnp.mean(dscaled * xs, axis=-1, keepdims=True))
    g = gout[...]
    fgrad[...] = (g.astype(F32) + dx).astype(BF16)

    def put(n, value):
        value = value.astype(BF16)
        wgrads[0, n * width : (n + 1) * width, :] = value[:, :half]
        wgrads[1, n * width : (n + 1) * width, :] = value[:, half:]

    for n, d in enumerate((dq, dk_t, dv_t)):
        put(n, mul(normed, d, 0, 1))
    put(3, mul(attn_t[...], g, 1, 0))
    put(4, mul(mean[...], g, 0, 0))


def gradients(nb, *args):
    normed_all, feat = args[0], args[3]
    total, width = normed_all.shape
    rows = feat.shape[0]
    vmem = pl.BlockSpec(memory_space=pltpu.VMEM)
    return pl.pallas_call(
        partial(gradient_kernel, nb),
        out_shape=[
            jax.ShapeDtypeStruct((rows, width), BF16),
            jax.ShapeDtypeStruct((2, 5 * width, width // 2), BF16),
            jax.ShapeDtypeStruct((8, width), F32),
        ],
        in_specs=[vmem] * len(args),
        out_specs=[vmem] * 3,
        scratch_shapes=[
            pltpu.VMEM((width, total), BF16),
            pltpu.VMEM((width, total), BF16),
            pltpu.VMEM((width, rows), BF16),
            pltpu.VMEM((width, rows), BF16),
            pltpu.VMEM((rows, total), F32),
            pltpu.VMEM((width, rows), F32),
            pltpu.VMEM((width, rows), F32),
        ],
        compiler_params=params(),
    )(*args)


def plan(nd, nb, rows):
    dom_bits = [1 << i for i in range(nd.bit_length() - 1)]
    blk_bits = [1 << i for i in range(nb.bit_length() - 1)]
    orders = (dom_bits, dom_bits[:1] + dom_bits[:0:-1])
    plans = []
    for order in orders:
        held, steps = rows, []
        for axis, bit in [("dom", b) for b in order] + [("blk", b) for b in blk_bits[::-1]]:
            halves = held % 32 == 0
            steps.append((axis, bit, held, halves))
            held = held // 2 if halves else held
        plans.append(steps)
    return plans


def reduce_kernel(plans, w, g, out, gsum, acc, gacc, *rest):
    n = len(plans[0])
    recvs, (grecv, send, recv, asend, arecv, gsend, grsem) = rest[: 2 * n], rest[2 * n :]
    index = {"dom": lax.axis_index("dom"), "blk": lax.axis_index("blk")}

    def bit_of(axis, bit):
        return lax.rem(index[axis] // bit, 2)

    def peer_of(axis, bit):
        return index[axis] + bit - 2 * bit * bit_of(axis, bit)

    barrier = pltpu.get_barrier_semaphore()
    for axis, bit, _, _ in plans[0]:
        pl.semaphore_signal(
            barrier, inc=1, device_id={axis: peer_of(axis, bit)}, device_id_type=MESH
        )
    pl.semaphore_wait(barrier, n)

    def rows_at(first, count):
        return pl.ds(pl.multiple_of(first, 16), count)

    gacc[0] = g[...]
    first = [0, 0]
    history = [[], []]
    for s in range(n):
        copies = []
        for half in range(2):
            axis, bit, held, halves = plans[half][s]
            mine = bit_of(axis, bit)
            peer = peer_of(axis, bit)
            count = held // 2 if halves else held
            away = first[half] + (1 - mine) * count if halves else first[half]
            keep = first[half] + mine * count if halves else first[half]
            src = (w if s == 0 else acc.at[s - 1]).at[half, rows_at(away, count), :]
            c = remote(src, recvs[2 * s + half], send.at[s, half], recv.at[s, half], axis, peer)
            c.start()
            copies.append((c, keep, count))
            history[half].append((axis, peer, keep, count, halves))
            first[half] = keep
        axis, bit, _, _ = plans[0][s]
        gc = remote(
            gacc.at[s], grecv.at[s], gsend.at[s], grsem.at[s], axis, peer_of(axis, bit)
        )
        gc.start()
        for half, (c, keep, count) in enumerate(copies):
            c.wait_recv()
            src = w if s == 0 else acc.at[s - 1]
            total = (
                src[half, rows_at(keep, count), :].astype(F32)
                + recvs[2 * s + half][...].astype(F32)
            ).astype(BF16)
            if s == n - 1:
                out[half, rows_at(keep, count), :] = total
            else:
                acc[s, half, rows_at(keep, count), :] = total
        gc.wait()
        gacc[s + 1] = gacc[s] + grecv[s]
        for c, _, _ in copies:
            c.wait_send()
    gsum[...] = gacc[n]
    for s in range(n - 1, -1, -1):
        copies = []
        for half in range(2):
            axis, peer, keep, count, halves = history[half][s]
            if not halves:
                continue
            place = out.at[half, rows_at(keep, count), :]
            c = remote(place, place, asend.at[s, half], arecv.at[s, half], axis, peer)
            c.start()
            copies.append(c)
        for c in copies:
            c.wait()


def reduce_all(nd, nb, w, g):
    plans = plan(nd, nb, w.shape[1])
    n = len(plans[0])
    vmem = pl.BlockSpec(memory_space=pltpu.VMEM)
    dma = pltpu.SemaphoreType.DMA
    bufs = []
    for s in range(n):
        for half in range(2):
            _, _, held, halves = plans[half][s]
            bufs.append(pltpu.VMEM((held // 2 if halves else held, w.shape[2]), BF16))
    return pl.pallas_call(
        partial(reduce_kernel, plans),
        out_shape=[
            jax.ShapeDtypeStruct(w.shape, BF16),
            jax.ShapeDtypeStruct(g.shape, F32),
        ],
        in_specs=[vmem] * 2,
        out_specs=[vmem] * 2,
        scratch_shapes=[
            pltpu.VMEM((n - 1,) + w.shape, BF16),
            pltpu.VMEM((n + 1,) + g.shape, F32),
        ]
        + bufs
        + [pltpu.VMEM((n,) + g.shape, F32)]
        + [dma((n, 2))] * 4
        + [dma((n,))] * 2,
        compiler_params=params(2),
    )(w, g)


def local(
    node_features, norm_gain, w_query, w_key, w_value, w_out, w_message, node_cluster,
    block_pattern, send_rows, send_counts, edge_src, edge_dst, out_grad,
):
    rows, width = node_features.shape
    nd = lax.axis_size("dom")
    nb = lax.axis_size("blk")
    me = lax.axis_index("blk")
    cap = send_rows.shape[1]
    gain = norm_gain.reshape(1, width)
    live = jnp.arange(cap, dtype=jnp.int32)[None, :] < send_counts[:, None]
    sidx = jnp.where(live, send_rows, -1)
    pattern_row = jnp.pad(block_pattern, ((0, 0), (0, rows - nb)))
    meta = jnp.concatenate(
        [node_cluster[None, :], pattern_row, jnp.zeros((6, rows), jnp.int32)], axis=0
    )
    feats, gouts, metas, mean, halo = exchange(
        nd, nb, node_features, out_grad, gain, w_message, meta, sidx,
        edge_src.reshape(-1, EDGE_PART), edge_dst.reshape(-1, EDGE_PART),
    )
    labels = metas[:, 0, :]
    key_labels = jnp.where(block_pattern[0][:, None] == 1, labels, -1).reshape(-1, 1)
    towards_me = lax.dynamic_slice_in_dim(metas[:, 1, :], me, 1, 1)
    query_labels = jnp.where(towards_me == 1, labels, -1).reshape(1, -1)
    feats = feats.reshape(nb * rows, width)
    gouts = gouts.reshape(nb * rows, width)
    layer_out, normed_all, attn_t, dq_t, stats = attend(
        feats, node_features, out_grad, gain, w_query, w_key, w_value, w_out, mean, w_message,
        key_labels, node_cluster.reshape(1, rows),
    )
    stats = share(nb, stats)
    feature_grad, wgrads, gain_part = gradients(
        nb, normed_all, gouts, stats, node_features, out_grad, gain, w_query, w_key, w_value,
        w_out, node_cluster.reshape(rows, 1), query_labels, attn_t, dq_t, mean, halo,
    )
    sums, gain_sum = reduce_all(nd, nb, wgrads, gain_part)
    sums = sums.astype(F32).reshape(2, 5, width, width // 2)
    weight_sums = jnp.concatenate([sums[0], sums[1]], axis=-1)
    return (layer_out, feature_grad, weight_sums, gain_sum[0])


def solution(mesh):
    nodes = P(("dom", "blk"))
    wide = P(("dom", "blk"), None)
    placed = (
        wide, P(), P(), P(), P(), P(), P(), nodes, wide, wide, nodes, nodes, nodes, wide,
    )
    return jax.shard_map(
        local,
        mesh=mesh,
        in_specs=placed,
        out_specs=(wide, wide, P(), P()),
        check_vma=False,
    )
```

```python
from functools import partial

import jax
import jax.numpy as jnp
from jax import lax
from jax.experimental import pallas as pl
from jax.experimental.pallas import tpu as pltpu
from jax.sharding import PartitionSpec as P

HEADS = 8
HEAD_DIM = 64
SCALE = 8.0 / HEAD_DIM
SHIFT = 8.0
EPS = 1e-06
MASKED = -1e30
EDGE_PART = 512
MESH = pl.DeviceIdType.MESH
F32 = jnp.float32
BF16 = jnp.bfloat16


def params(collective_id=None):
    return pltpu.CompilerParams(
        vmem_limit_bytes=56 * 1024 * 1024,
        collective_id=collective_id,
        has_side_effects=collective_id is not None,
    )


def mul(a, b, ca, cb):
    return lax.dot_general(a, b, (((ca,), (cb,)), ((), ())), preferred_element_type=F32)


def row_scale(x):
    return lax.rsqrt(jnp.mean(x * x, axis=-1, keepdims=True) + EPS)


def head_norm(x):
    view = x.reshape(HEADS, HEAD_DIM, x.shape[1])
    scaling = lax.rsqrt(jnp.mean(view * view, axis=1, keepdims=True) + EPS)
    return view * scaling, scaling


def head_norm_pull(y, scaling, dy):
    dy = dy.reshape(y.shape)
    dx = scaling * (dy - y * jnp.mean(y * dy, axis=1, keepdims=True))
    return dx.reshape(-1, y.shape[2])


def remote(src, dst, send, recv, axis, peer):
    return pltpu.make_async_remote_copy(
        src_ref=src, dst_ref=dst, send_sem=send, recv_sem=recv,
        device_id={axis: peer}, device_id_type=MESH,
    )


def plan(nd, nb, rows, flip):
    dom_bits = [1 << i for i in range(nd.bit_length() - 1)]
    blk_bits = [1 << i for i in range(nb.bit_length() - 1)]
    if flip:
        dom_bits = dom_bits[:1] + dom_bits[:0:-1]
    steps = []
    for axis, bit in [("dom", b) for b in dom_bits] + [("blk", b) for b in blk_bits]:
        halves = rows % 32 == 0
        rows = rows // 2 if halves else rows
        steps.append((axis, bit, rows, halves))
    return steps


FLIPS = (True, False, True, False, True)
PIECES = len(FLIPS)


def layer_kernel(
    nd, nb,
    feat, gout, gain, wq, wk, wv, wo, wm, labels, sidx, esrc, edst, live_counts, pattern,
    layer, fgrad, sums, gsum,
    feats, gouts, metas, mine, sbuf, rbuf, sback, rback, cnt, onehot,
    k_t, v_t, q_t, q_own, ga_t, attn_t, mean_rows, bias, bias_own, dq_f, dk_f, dv_f, gh_t,
    stats, all_stats, terms, gacc, grecv,
    zsend, zrecv, asend, arecv, bsend, brecv, ssend, srecv,
    rsend, rrecv, gsend, grsem, hsend, hrecv,
    *buffers,
):
    me = lax.axis_index("blk")
    my_dom = lax.axis_index("dom")
    index = {"dom": my_dom, "blk": me}
    rows, width = feat.shape
    cap = sidx.shape[1]
    plans = [plan(nd, nb, width, f) for f in FLIPS]
    n = len(plans[0])
    acc = [[buffers[2 * (p * n + s)] for s in range(n)] for p in range(PIECES)]
    got = [[buffers[2 * (p * n + s) + 1] for s in range(n)] for p in range(PIECES)]

    barrier = pltpu.get_barrier_semaphore()
    for axis, size in (("dom", nd), ("blk", nb)):
        for k in range(1, size):
            pl.semaphore_signal(
                barrier, inc=1, device_id={axis: lax.rem(index[axis] + k, size)},
                device_id_type=MESH,
            )

    own_labels = labels[...]
    mine[...] = jnp.zeros_like(mine)
    mine[0:1, :] = own_labels
    for b in range(nb):
        mine[1 + b : 2 + b, :] = jnp.where(pattern[0, b] == 1, own_labels, -1)
    pl.semaphore_wait(barrier, nd - 1 + nb - 1)

    streams = ((feat, feats), (gout, gouts), (mine, metas))

    def line_copy(step, way, k, block):
        src, dst = streams[k]
        if step > 0:
            src = dst.at[block]
        peer = me + 1 if way == 0 else me - 1
        return remote(
            src, dst.at[block], zsend.at[way, step, k], zrecv.at[way, step, k], "blk", peer
        )

    def line_send(step, kinds, start=True):
        for way in range(2):
            sends = (me + 1 < nb) & (me - step >= 0) if way == 0 else (me >= 1) & (me + step < nb)
            block = me - step if way == 0 else me + step

            @pl.when(sends)
            def _():
                for k in kinds:
                    c = line_copy(step, way, k, block)
                    if start:
                        c.start()
                    else:
                        c.wait_send()

    def line_recv(step, kinds):
        for way in range(2):
            block = me - 1 - step if way == 0 else me + 1 + step
            comes = block >= 0 if way == 0 else block < nb

            @pl.when(comes)
            def _():
                for k in kinds:
                    line_copy(step, way, k, block).wait_recv()

    def swap(src, dst, send, recv, k, incoming):
        to = lax.rem(my_dom + k, nd)
        origin = lax.rem(my_dom + nd - k, nd)
        return remote(
            src.at[to], dst.at[origin if incoming else my_dom], send.at[k], recv.at[k], "dom", to
        )

    stage = [-1] * PIECES
    first = [None] * PIECES
    history = [[] for _ in range(PIECES)]

    def aligned(start, count):
        return pl.ds(pl.multiple_of(start, 16), count)

    def peer_of(axis, bit):
        mine_bit = lax.rem(index[axis] // bit, 2)
        return mine_bit, index[axis] + bit - 2 * bit * mine_bit

    def gain_copy(s):
        axis, bit, _, _ = plans[1][s]
        return remote(gacc.at[s], grecv.at[s], gsend.at[s], grsem.at[s], axis, peer_of(axis, bit)[1])

    def reduce_copy(p, s):
        axis, bit, count, halves = plans[p][s]
        bit_set, peer = peer_of(axis, bit)
        src = terms.at[p] if s == 0 else acc[p][s - 1]
        away = (1 - bit_set) * count if halves else 0
        keep = bit_set * count if halves else 0
        c = remote(
            src.at[aligned(away, count), :], got[p][s], rsend.at[p, s], rrecv.at[p, s], axis, peer
        )
        return c, src, keep

    def spread_copy(p, s):
        axis, peer, start, count = history[p][s]
        place = sums.at[aligned(p * width + start, count), :]
        return remote(place, place, hsend.at[p, s], hrecv.at[p, s], axis, peer)

    def begin(p):
        stage[p] = 0
        first[p] = 0
        reduce_copy(p, 0)[0].start()

    def advance(p):
        s = stage[p]
        if s < n:
            c, src, keep = reduce_copy(p, s)
            axis, bit, count, halves = plans[p][s]
            c.wait_recv()
            total = (
                src[aligned(keep, count), :].astype(F32) + got[p][s][...].astype(F32)
            ).astype(BF16)
            first[p] = first[p] + keep
            history[p].append((axis, peer_of(axis, bit)[1], first[p], count))
            if s == n - 1:
                sums[aligned(p * width + first[p], count), :] = total
            else:
                acc[p][s][...] = total
                reduce_copy(p, s + 1)[0].start()
        else:
            spread_copy(p, 2 * n - 1 - s).wait_recv()
        s += 1
        while n <= s < 2 * n and not plans[p][2 * n - 1 - s][3]:
            s += 1
        stage[p] = s
        if n <= s < 2 * n:
            spread_copy(p, 2 * n - 1 - s).start()

    def advance_if(p):
        if 0 <= stage[p] < 2 * n:
            advance(p)

    def settle(p):
        for s in range(n):
            reduce_copy(p, s)[0].wait_send()
            if plans[p][s][3]:
                spread_copy(p, s).wait_send()

    line_send(0, (0, 2))
    feats[me] = feat[...]
    gouts[me] = gout[...]
    metas[me] = mine[...]

    x = feat[...].astype(F32)
    scaling = row_scale(x)
    normed = (x * scaling * gain[...]).astype(BF16)
    row_ids = lax.broadcasted_iota(jnp.int32, (rows, cap), 0)
    lane_ids = lax.broadcasted_iota(jnp.int32, (1, cap), 1)
    for p in range(nd):
        picks = jnp.where(lane_ids < live_counts[p], sidx[p : p + 1, :], -1)
        hot = jnp.where(row_ids == picks, 1.0, 0.0).astype(BF16)
        onehot[:, p * cap : (p + 1) * cap] = hot
        sbuf[p] = mul(hot, normed, 0, 0).astype(BF16)
    for k in range(1, nd):
        swap(sbuf, rbuf, asend, arecv, k, False).start()
    rbuf[my_dom] = sbuf[my_dom]

    slot_ids = lax.broadcasted_iota(jnp.int32, (nd * cap, EDGE_PART), 0)
    dst_ids = lax.broadcasted_iota(jnp.int32, (rows, EDGE_PART), 0)
    cnt[...] = jnp.zeros_like(cnt)

    def count_edges(c, carry):
        at = pl.ds(pl.multiple_of(c * EDGE_PART, EDGE_PART), EDGE_PART)
        hot_src = jnp.where(slot_ids == esrc[:, at], 1.0, 0.0).astype(BF16)
        hot_dst = jnp.where(dst_ids == edst[:, at], 1.0, 0.0).astype(BF16)
        cnt[...] += mul(hot_dst, hot_src, 1, 1)
        return carry

    lax.fori_loop(0, esrc.shape[1] // EDGE_PART, count_edges, 0)
    counts = cnt[...]
    degree = jnp.maximum(jnp.sum(counts, axis=1, keepdims=True), 1.0)
    counts = counts.astype(BF16)
    if nb > 2:
        line_recv(0, (0, 2))
        line_send(1, (0, 2))
    dmessage = (mul(gout[...], wm[...], 1, 1) / degree).astype(BF16)
    for p in range(nd):
        sback[p] = mul(counts[:, p * cap : (p + 1) * cap], dmessage, 0, 0).astype(BF16)
    for k in range(1, nd):
        swap(sback, rback, bsend, brecv, k, False).start()
    rback[my_dom] = sback[my_dom]

    queries, q_scaling = head_norm(mul(wq[...], normed, 0, 1))
    q_own[...] = (queries * SCALE).reshape(q_own.shape).astype(BF16)
    ga_t[...] = mul(wo[...], gout[...], 1, 1)
    for k in range(1, nd):
        swap(sbuf, rbuf, asend, arecv, k, True).wait_recv()
    mean = (mul(counts, rbuf[...].reshape(nd * cap, width), 1, 0) / degree).astype(BF16)
    mean_rows[...] = mean
    terms[4] = mul(mean, gout[...], 0, 0).astype(BF16)
    begin(4)
    for step in range(2, nb - 1):
        line_recv(step - 1, (0, 2))
        line_send(step, (0, 2))
    line_recv(nb - 2, (0, 2))
    line_send(0, (1,))

    x_all = feats[...].reshape(nb * rows, width).astype(F32)
    normed_all = (x_all * row_scale(x_all) * gain[...]).astype(BF16)
    keys, _ = head_norm(mul(wk[...], normed_all, 0, 1))
    k_t[...] = keys.reshape(k_t.shape).astype(BF16)
    v_t[...] = mul(wv[...], normed_all, 0, 1).astype(BF16)
    all_queries, _ = head_norm(mul(wq[...], normed_all, 0, 1))
    q_t[...] = (all_queries * SCALE).reshape(q_t.shape).astype(BF16)
    own_row = own_labels.astype(F32)
    own_column = jnp.broadcast_to(own_row, (rows, rows)).T
    for b in range(nb):
        at = slice(b * rows, (b + 1) * rows)
        row = jnp.where(pattern[0, b] == 1, metas[b, 0:1, :], -1).astype(F32)
        column = jnp.broadcast_to(row, (rows, rows)).T
        bias[at, :] = jnp.where(column == own_row, -SHIFT, MASKED)
        towards = metas[b, pl.ds(1 + me, 1), :].astype(F32)
        bias_own[:, at] = jnp.where(own_column == towards, -SHIFT, MASKED)
    pending = list(range(1, nb - 1))
    for h in range(HEADS):
        part = slice(h * HEAD_DIM, (h + 1) * HEAD_DIM)
        kh, vh, qh, ga = k_t[part, :], v_t[part, :], q_own[part, :], ga_t[part, :]
        weights = jnp.exp(mul(kh, qh, 0, 0) + bias[...])
        inv = 1.0 / jnp.sum(weights, axis=0, keepdims=True)
        attn = (mul(vh, weights.astype(BF16), 1, 0) * inv).astype(BF16)
        attn_t[part, :] = attn
        correction = jnp.sum(ga * attn.astype(F32), axis=0, keepdims=True) * inv
        stats[h : h + 1, :] = inv
        stats[HEADS + h : HEADS + h + 1, :] = correction
        dots = mul(vh, (ga * inv).astype(BF16), 0, 0)
        slopes = (weights * (dots - correction)).astype(BF16)
        dq_f[part, :] = mul(kh, slopes, 1, 0) * SCALE
        if h % 2 == 1:
            advance_if(4)
        if h % 3 == 2 and pending:
            step = pending.pop(0)
            line_recv(step - 1, (1,))
            line_send(step, (1,))
    for step in pending:
        line_recv(step - 1, (1,))
        line_send(step, (1,))
    for k in range(1, nb):
        to = lax.rem(me + k, nb)
        remote(stats, all_stats.at[me], ssend.at[k], srecv.at[k], "blk", to).start()
    all_stats[me] = stats[...]
    dq = head_norm_pull(queries, q_scaling, dq_f[...]).astype(BF16)
    terms[3] = mul(attn_t[...], gout[...], 1, 0).astype(BF16)
    begin(3)
    terms[0] = mul(normed, dq, 0, 1).astype(BF16)
    begin(0)
    out = x + mul(mean_rows[...], wm[...], 1, 0) + mul(attn_t[...], wo[...], 0, 0)
    layer[...] = out.astype(BF16)
    for k in range(1, nd):
        swap(sback, rback, bsend, brecv, k, True).wait_recv()
    halo = mul(onehot[...], rback[...].reshape(nd * cap, width), 1, 0)

    own_keys, k_scaling = head_norm(mul(wk[...], normed, 0, 1))
    k_own = own_keys.reshape(width, rows).astype(BF16)
    v_own = mul(wv[...], normed, 0, 1).astype(BF16)
    line_recv(nb - 2, (1,))
    for k in range(1, nb):
        to = lax.rem(me + k, nb)
        origin = lax.rem(me + nb - k, nb)
        remote(stats, all_stats.at[origin], ssend.at[k], srecv.at[k], "blk", to).wait()
    inv_all = jnp.concatenate([all_stats[b, :HEADS, :] for b in range(nb)], axis=1)
    corrections = jnp.concatenate([all_stats[b, HEADS:, :] for b in range(nb)], axis=1)
    ga_all = mul(wo[...], gouts[...].reshape(nb * rows, width), 1, 1)
    ga_all = ga_all.reshape(HEADS, HEAD_DIM, nb * rows) * inv_all[:, None, :]
    gh_t[...] = ga_all.reshape(gh_t.shape).astype(BF16)
    advance_if(4)
    for h in range(HEADS):
        part = slice(h * HEAD_DIM, (h + 1) * HEAD_DIM)
        kh, vh, qh, gh = k_own[part, :], v_own[part, :], q_t[part, :], gh_t[part, :]
        weights = jnp.exp(mul(kh, qh, 0, 0) + bias_own[...])
        dots = mul(vh, gh, 0, 0)
        slopes = (weights * (dots - corrections[h : h + 1, :])).astype(BF16)
        dk_f[part, :] = mul(qh, slopes, 1, 1)
        dv_f[part, :] = mul(gh, weights.astype(BF16), 1, 1)
        if h % 2 == 0:
            advance_if(4)
        else:
            advance_if(3)
            advance_if(0)
    dk = head_norm_pull(own_keys, k_scaling, dk_f[...]).astype(BF16)
    dv = dv_f[...].astype(BF16)
    terms[1] = mul(normed, dk, 0, 1).astype(BF16)
    begin(1)
    terms[2] = mul(normed, dv, 0, 1).astype(BF16)
    begin(2)
    for p in (4, 3, 0):
        advance_if(p)
    dnormed = (mul(wq[...], dq, 1, 0) + mul(wk[...], dk, 1, 0) + mul(wv[...], dv, 1, 0)).T
    dnormed = dnormed + halo
    xs = x * scaling
    gacc[0] = jnp.broadcast_to(jnp.sum(dnormed * xs, axis=0, keepdims=True), gacc.shape[1:])
    gain_copy(0).start()
    dscaled = dnormed * gain[...]
    dx = scaling * (dscaled - xs * jnp.mean(dscaled * xs, axis=-1, keepdims=True))
    fgrad[...] = (gout[...].astype(F32) + dx).astype(BF16)
    turn = 0
    while any(stage[p] < 2 * n for p in range(PIECES)):
        for p in (1, 2, 3, 0, 4):
            advance_if(p)
        if turn < n:
            gain_copy(turn).wait()
            gacc[turn + 1] = gacc[turn] + grecv[turn]
            if turn + 1 < n:
                gain_copy(turn + 1).start()
        turn += 1
    gsum[...] = gacc[n]

    for p in range(PIECES):
        settle(p)
    for step in range(nb - 1):
        line_send(step, (0, 1, 2), False)
    for k in range(1, nd):
        swap(sbuf, rbuf, asend, arecv, k, False).wait_send()
        swap(sback, rback, bsend, brecv, k, False).wait_send()


def layer_call(nd, nb, *args):
    feat, sidx = args[0], args[9]
    rows, width = feat.shape
    cap = sidx.shape[1]
    total, slots = nb * rows, nd * cap
    vmem = pl.BlockSpec(memory_space=pltpu.VMEM)
    smem = pl.BlockSpec(memory_space=pltpu.SMEM)
    dma = pltpu.SemaphoreType.DMA
    V = pltpu.VMEM
    n = len(plan(nd, nb, width, False))
    buffers = []
    for flip in FLIPS:
        for _, _, count, _ in plan(nd, nb, width, flip):
            buffers += [V((count, width), BF16)] * 2
    return pl.pallas_call(
        partial(layer_kernel, nd, nb),
        out_shape=[
            jax.ShapeDtypeStruct((rows, width), BF16),
            jax.ShapeDtypeStruct((rows, width), BF16),
            jax.ShapeDtypeStruct((PIECES * width, width), BF16),
            jax.ShapeDtypeStruct((8, width), F32),
        ],
        in_specs=[vmem] * 12 + [smem] * 2,
        out_specs=[vmem] * 4,
        scratch_shapes=[
            V((nb, rows, width), BF16), V((nb, rows, width), BF16),
            V((nb, 16, rows), jnp.int32), V((16, rows), jnp.int32),
            V((nd, cap, width), BF16), V((nd, cap, width), BF16),
            V((nd, cap, width), BF16), V((nd, cap, width), BF16),
            V((rows, slots), F32), V((rows, slots), BF16),
            V((width, total), BF16), V((width, total), BF16), V((width, total), BF16),
            V((width, rows), BF16), V((width, rows), F32), V((width, rows), BF16),
            V((rows, width), BF16),
            V((total, rows), F32), V((rows, total), F32),
            V((width, rows), F32), V((width, rows), F32), V((width, rows), F32),
            V((width, total), BF16),
            V((2 * HEADS, rows), F32), V((nb, 2 * HEADS, rows), F32),
            V((PIECES, width, width), BF16),
            V((n + 1, 8, width), F32), V((n, 8, width), F32),
            dma((2, nb, 3)), dma((2, nb, 3)),
            dma((nd,)), dma((nd,)), dma((nd,)), dma((nd,)), dma((nb,)), dma((nb,)),
            dma((PIECES, n)), dma((PIECES, n)), dma((n,)), dma((n,)),
            dma((PIECES, n)), dma((PIECES, n)),
        ]
        + buffers,
        compiler_params=params(0),
    )(*args)


def local(
    node_features, norm_gain, w_query, w_key, w_value, w_out, w_message, node_cluster,
    block_pattern, send_rows, send_counts, edge_src, edge_dst, out_grad,
):
    rows, width = node_features.shape
    nd = lax.axis_size("dom")
    nb = lax.axis_size("blk")
    layer_out, feature_grad, sums, gain_sum = layer_call(
        nd, nb, node_features, out_grad, norm_gain.reshape(1, width),
        w_query, w_key, w_value, w_out, w_message, node_cluster.reshape(1, rows), send_rows,
        edge_src.reshape(1, -1), edge_dst.reshape(1, -1), send_counts, block_pattern,
    )
    weight_sums = sums.reshape(PIECES, width, width).astype(F32)
    return (layer_out, feature_grad, weight_sums, gain_sum[0])


def solution(mesh):
    nodes = P(("dom", "blk"))
    wide = P(("dom", "blk"), None)
    placed = (
        wide, P(), P(), P(), P(), P(), P(), nodes, wide, wide, nodes, nodes, nodes, wide,
    )
    return jax.shard_map(
        local,
        mesh=mesh,
        in_specs=placed,
        out_specs=(wide, wide, P(), P()),
        check_vma=False,
    )
```

```python
from functools import partial

import jax
import jax.numpy as jnp
from jax import lax
from jax.experimental import pallas as pl
from jax.experimental.pallas import tpu as pltpu
from jax.sharding import PartitionSpec as P

HEADS = 8
HEAD_DIM = 64
SCALE = 8.0 / HEAD_DIM
SHIFT = 8.0
EPS = 1e-06
MASKED = -1e30
EDGE_PART = 512
MESH = pl.DeviceIdType.MESH
F32 = jnp.float32
BF16 = jnp.bfloat16


def params(collective_id=None):
    return pltpu.CompilerParams(
        vmem_limit_bytes=56 * 1024 * 1024,
        collective_id=collective_id,
        has_side_effects=collective_id is not None,
    )


def mul(a, b, ca, cb):
    return lax.dot_general(a, b, (((ca,), (cb,)), ((), ())), preferred_element_type=F32)


def row_scale(x):
    return lax.rsqrt(jnp.mean(x * x, axis=-1, keepdims=True) + EPS)


def head_norm(x):
    view = x.reshape(HEADS, HEAD_DIM, x.shape[1])
    scaling = lax.rsqrt(jnp.mean(view * view, axis=1, keepdims=True) + EPS)
    return view * scaling, scaling


def head_norm_pull(y, scaling, dy):
    dy = dy.reshape(y.shape)
    dx = scaling * (dy - y * jnp.mean(y * dy, axis=1, keepdims=True))
    return dx.reshape(-1, y.shape[2])


def remote(src, dst, send, recv, axis, peer):
    return pltpu.make_async_remote_copy(
        src_ref=src, dst_ref=dst, send_sem=send, recv_sem=recv,
        device_id={axis: peer}, device_id_type=MESH,
    )


def plan(nd, rows, flip):
    bits = [1 << i for i in range(nd.bit_length() - 1)]
    if flip:
        bits = bits[:1] + bits[:0:-1]
    steps = []
    for bit in bits:
        halves = rows % 32 == 0
        rows = rows // 2 if halves else rows
        steps.append((bit, rows, halves))
    return steps


def line_rows(nb, rows):
    return rows // nb if rows % (16 * nb) == 0 else rows


FLIPS = (True, False, True, False, True)
PIECES = len(FLIPS)


def layer_kernel(
    nd, nb,
    feat, gout, gain, wq, wk, wv, wo, wm, labels, sidx, esrc, edst, live_counts, pattern,
    layer, fgrad, sums, gsum,
    feats, gouts, metas, mine, sbuf, rbuf, sback, rback, cnt, onehot,
    k_t, v_t, q_t, q_own, ga_t, attn_t, mean_rows, bias, bias_own, dq_f, dk_f, dv_f, gh_t, k_own_t, v_own_t,
    stats, all_stats, terms, gacc, grecv,
    zsend, zrecv, asend, arecv, bsend, brecv, ssend, srecv,
    rsend, rrecv, gsend, grsem, hsend, hrecv, lsend, lrecv, tsend, trecv, usend, urecv, gline,
    w_all, num, den,
    *buffers,
):
    me = lax.axis_index("blk")
    my_dom = lax.axis_index("dom")
    index = {"dom": my_dom, "blk": me}
    rows, width = feat.shape
    cap = sidx.shape[1]
    plans = [plan(nd, width, f) for f in FLIPS]
    n = len(plans[0])
    acc = [[buffers[2 * (p * n + s)] for s in range(n)] for p in range(PIECES)]
    last = plans[0][-1][1]
    share = line_rows(nb, last)
    stages = 2 * n + 2 if share < last else 2 * n + 1
    gline_in = buffers[-PIECES:]
    got = [[buffers[2 * (p * n + s) + 1] for s in range(n)] for p in range(PIECES)]

    barrier = pltpu.get_barrier_semaphore()
    for axis, size in (("dom", nd), ("blk", nb)):
        for k in range(1, size):
            pl.semaphore_signal(
                barrier, inc=1, device_id={axis: lax.rem(index[axis] + k, size)},
                device_id_type=MESH,
            )

    own_labels = labels[...]
    mine[...] = jnp.zeros_like(mine)
    mine[0:1, :] = own_labels
    for b in range(nb):
        mine[1 + b : 2 + b, :] = jnp.where(pattern[0, b] == 1, own_labels, -1)
    pl.semaphore_wait(barrier, nd - 1 + nb - 1)

    streams = ((feat, feats), (gout, gouts), (mine, metas))

    def line_copy(step, way, k, block):
        src, dst = streams[k]
        if step > 0:
            src = dst.at[block]
        peer = me + 1 if way == 0 else me - 1
        return remote(
            src, dst.at[block], zsend.at[way, step, k], zrecv.at[way, step, k], "blk", peer
        )

    def line_send(step, kinds, start=True):
        for way in range(2):
            sends = (me + 1 < nb) & (me - step >= 0) if way == 0 else (me >= 1) & (me + step < nb)
            block = me - step if way == 0 else me + step

            @pl.when(sends)
            def _():
                for k in kinds:
                    c = line_copy(step, way, k, block)
                    if start:
                        c.start()
                    else:
                        c.wait_send()

    def line_recv(step, kinds):
        for way in range(2):
            block = me - 1 - step if way == 0 else me + 1 + step
            comes = block >= 0 if way == 0 else block < nb

            @pl.when(comes)
            def _():
                for k in kinds:
                    line_copy(step, way, k, block).wait_recv()

    def swap(src, dst, send, recv, k, incoming):
        to = lax.rem(my_dom + k, nd)
        origin = lax.rem(my_dom + nd - k, nd)
        return remote(
            src.at[to], dst.at[origin if incoming else my_dom], send.at[k], recv.at[k], "dom", to
        )

    stage = [-1] * PIECES
    first = [None] * PIECES
    history = [[] for _ in range(PIECES)]

    def aligned(start, count):
        return pl.ds(pl.multiple_of(start, 16), count)

    def peer_of(axis, bit):
        mine_bit = lax.rem(index[axis] // bit, 2)
        return mine_bit, index[axis] + bit - 2 * bit * mine_bit

    def gain_copy(s):
        bit, _, _ = plans[1][s]
        return remote(
            gacc.at[s], grecv.at[s], gsend.at[s], grsem.at[s], "dom", peer_of("dom", bit)[1]
        )

    def gain_line(k, incoming):
        to = lax.rem(me + k, nb)
        origin = lax.rem(me + nb - k, nb)
        return remote(
            gacc.at[n], gline.at[origin if incoming else me], usend.at[k], urecv.at[k], "blk", to
        )

    def gain_turn(turn):
        if turn < n:
            gain_copy(turn).wait()
            gacc[turn + 1] = gacc[turn] + grecv[turn]
            if turn + 1 < n:
                gain_copy(turn + 1).start()
            else:
                for k in range(1, nb):
                    gain_line(k, False).start()
                gline[me] = gacc[n]
        elif turn == n:
            for k in range(1, nb):
                gain_line(k, True).wait()
            total = gline[0]
            for b in range(1, nb):
                total = total + gline[b]
            gsum[...] = total[0:1, :]

    def reduce_copy(p, s):
        bit, count, halves = plans[p][s]
        bit_set, peer = peer_of("dom", bit)
        src = terms.at[p] if s == 0 else acc[p][s - 1]
        away = (1 - bit_set) * count if halves else 0
        keep = bit_set * count if halves else 0
        c = remote(
            src.at[aligned(away, count), :], got[p][s], rsend.at[p, s], rrecv.at[p, s], "dom", peer
        )
        return c, src, keep

    def share_of(b):
        return aligned(b * share, share) if share < last else aligned(0, last)

    def line_reduce(p, k, incoming):
        to = lax.rem(me + k, nb)
        origin = lax.rem(me + nb - k, nb)
        return remote(
            acc[p][n - 1].at[share_of(to), :],
            gline_in[p].at[origin if incoming else me],
            lsend.at[p, k], lrecv.at[p, k], "blk", to,
        )

    def line_spread(p, k, incoming):
        to = lax.rem(me + k, nb)
        origin = lax.rem(me + nb - k, nb)
        src = sums.at[aligned(p * width + first[p] + me * share, share), :]
        dst = sums.at[aligned(p * width + first[p] + (origin if incoming else me) * share, share), :]
        return remote(src, dst, tsend.at[p, k], trecv.at[p, k], "blk", to)

    def spread_copy(p, s):
        peer, start, count = history[p][s]
        place = sums.at[aligned(p * width + start, count), :]
        return remote(place, place, hsend.at[p, s], hrecv.at[p, s], "dom", peer)

    def back_step(p, stage_now):
        return stages - 1 - stage_now

    def launch(p):
        s = stage[p]
        if s < n:
            reduce_copy(p, s)[0].start()
        elif s == n:
            for k in range(1, nb):
                line_reduce(p, k, False).start()
            gline_in[p][me] = acc[p][n - 1][share_of(me), :]
        elif s < stages - n:
            for k in range(1, nb):
                line_spread(p, k, False).start()
        elif s < stages:
            spread_copy(p, back_step(p, s)).start()

    def begin(p):
        stage[p] = 0
        first[p] = 0
        launch(p)

    def advance(p):
        s = stage[p]
        if s < n:
            c, src, keep = reduce_copy(p, s)
            bit, count, halves = plans[p][s]
            c.wait_recv()
            total = src[aligned(keep, count), :].astype(F32) + got[p][s][...].astype(F32)
            first[p] = first[p] + keep
            history[p].append((peer_of("dom", bit)[1], first[p], count))
            acc[p][s][...] = total.astype(BF16)
        elif s == n:
            for k in range(1, nb):
                line_reduce(p, k, True).wait_recv()
            total = gline_in[p][0].astype(F32)
            for b in range(1, nb):
                total = total + gline_in[p][b].astype(F32)
            mine_at = me * share if share < last else 0
            sums[aligned(p * width + first[p] + mine_at, share), :] = total.astype(BF16)
        elif s < stages - n:
            for k in range(1, nb):
                line_spread(p, k, True).wait_recv()
        else:
            spread_copy(p, back_step(p, s)).wait_recv()
        s += 1
        while stages - n <= s < stages and not plans[p][back_step(p, s)][2]:
            s += 1
        stage[p] = s
        launch(p)

    def advance_if(p):
        if 0 <= stage[p] < stages:
            advance(p)

    def settle(p):
        for s in range(n):
            reduce_copy(p, s)[0].wait_send()
            if plans[p][s][2]:
                spread_copy(p, s).wait_send()
        for k in range(1, nb):
            line_reduce(p, k, False).wait_send()
            if share < last:
                line_spread(p, k, False).wait_send()

    line_send(0, (0, 2))
    feats[me] = feat[...]
    gouts[me] = gout[...]
    metas[me] = mine[...]

    x = feat[...].astype(F32)
    scaling = row_scale(x)
    normed = (x * scaling * gain[...]).astype(BF16)
    row_ids = lax.broadcasted_iota(jnp.int32, (rows, cap), 0)
    lane_ids = lax.broadcasted_iota(jnp.int32, (1, cap), 1)
    for p in range(nd):
        picks = jnp.where(lane_ids < live_counts[p], sidx[p : p + 1, :], -1)
        hot = jnp.where(row_ids == picks, 1.0, 0.0).astype(BF16)
        onehot[:, p * cap : (p + 1) * cap] = hot
        sbuf[p] = mul(hot, normed, 0, 0).astype(BF16)
    for k in range(1, nd):
        swap(sbuf, rbuf, asend, arecv, k, False).start()
    rbuf[my_dom] = sbuf[my_dom]

    slot_ids = lax.broadcasted_iota(jnp.int32, (nd * cap, EDGE_PART), 0)
    dst_ids = lax.broadcasted_iota(jnp.int32, (rows, EDGE_PART), 0)
    cnt[...] = jnp.zeros_like(cnt)

    def count_edges(c, carry):
        at = pl.ds(pl.multiple_of(c * EDGE_PART, EDGE_PART), EDGE_PART)
        hot_src = jnp.where(slot_ids == esrc[:, at], 1.0, 0.0).astype(BF16)
        hot_dst = jnp.where(dst_ids == edst[:, at], 1.0, 0.0).astype(BF16)
        cnt[...] += mul(hot_dst, hot_src, 1, 1)
        return carry

    lax.fori_loop(0, esrc.shape[1] // EDGE_PART, count_edges, 0)
    counts = cnt[...]
    degree = jnp.maximum(jnp.sum(counts, axis=1, keepdims=True), 1.0)
    counts = counts.astype(BF16)
    if nb > 2:
        line_recv(0, (0, 2))
        line_send(1, (0, 2))
    dmessage = (mul(gout[...], wm[...], 1, 1) / degree).astype(BF16)
    for p in range(nd):
        sback[p] = mul(counts[:, p * cap : (p + 1) * cap], dmessage, 0, 0).astype(BF16)
    for k in range(1, nd):
        swap(sback, rback, bsend, brecv, k, False).start()
    rback[my_dom] = sback[my_dom]

    own_row = own_labels.astype(F32)
    own_column = jnp.broadcast_to(own_row, (rows, rows)).T
    queries, q_scaling = head_norm(mul(wq[...], normed, 0, 1))
    q_own[...] = (queries * SCALE).reshape(q_own.shape).astype(BF16)
    ga_t[...] = mul(wo[...], gout[...], 1, 1)
    num[...] = jnp.zeros_like(num)
    den[...] = jnp.zeros_like(den)

    def heads(body):
        def pair(i, carry):
            for j in range(2):
                h = 2 * i + j
                body(h, pl.ds(pl.multiple_of(h * HEAD_DIM, HEAD_DIM), HEAD_DIM))
            return carry

        lax.fori_loop(0, HEADS // 2, pair, 0)

    def forward(block):
        at = pl.ds(pl.multiple_of(block * rows, rows), rows)
        xb = feats[block].astype(F32)
        nb_rows = (xb * row_scale(xb) * gain[...]).astype(BF16)
        keys, _ = head_norm(mul(wk[...], nb_rows, 0, 1))
        k_t[:, at] = keys.reshape(width, rows).astype(BF16)
        v_t[:, at] = mul(wv[...], nb_rows, 0, 1).astype(BF16)
        block_queries, _ = head_norm(mul(wq[...], nb_rows, 0, 1))
        q_t[:, at] = (block_queries * SCALE).reshape(width, rows).astype(BF16)
        column = jnp.broadcast_to(metas[block, 0:1, :].astype(F32), (rows, rows)).T
        seen = jnp.where(pattern[0, block] == 1, own_row, -1.0)
        bias[...] = jnp.where(column == seen, -SHIFT, MASKED)
        towards = metas[block, pl.ds(1 + me, 1), :].astype(F32)
        bias_own[:, at] = jnp.where(own_column == towards, -SHIFT, MASKED)

        def one(h, part):
            weights = jnp.exp(mul(k_t[part, at], q_own[part, :], 0, 0) + bias[...])
            den[pl.ds(h, 1), :] += jnp.sum(weights, axis=0, keepdims=True)
            weights = weights.astype(BF16)
            w_all[h, at, :] = weights
            num[part, :] += mul(v_t[part, at], weights, 1, 0)

        heads(one)

    def at_distance(distance, body):
        for way in range(2):
            block = me - distance if way == 0 else me + distance

            @pl.when(block >= 0 if way == 0 else block < nb)
            def _():
                body(block)

    forward(me)
    for k in range(1, nd):
        swap(sbuf, rbuf, asend, arecv, k, True).wait_recv()
    mean = (mul(counts, rbuf[...].reshape(nd * cap, width), 1, 0) / degree).astype(BF16)
    mean_rows[...] = mean
    terms[4] = mul(mean, gout[...], 0, 0).astype(BF16)
    begin(4)
    for step in range(2, nb - 1):
        line_recv(step - 1, (0, 2))
        line_send(step, (0, 2))
        at_distance(step - 1, forward)
        advance_if(4)
    line_recv(nb - 2, (0, 2))
    line_send(0, (1,))
    for distance in range(max(nb - 2, 1), nb):
        at_distance(distance, forward)
        advance_if(4)

    pending = list(range(1, nb - 1))
    for h in range(HEADS):
        part = slice(h * HEAD_DIM, (h + 1) * HEAD_DIM)
        kh, vh, ga = k_t[part, :], v_t[part, :], ga_t[part, :]
        inv = 1.0 / den[h : h + 1, :]
        attn = (num[part, :] * inv).astype(BF16)
        attn_t[part, :] = attn
        correction = jnp.sum(ga * attn.astype(F32), axis=0, keepdims=True) * inv
        stats[h : h + 1, :] = inv
        stats[HEADS + h : HEADS + h + 1, :] = correction
        dots = mul(vh, (ga * inv).astype(BF16), 0, 0)
        slopes = (w_all[h].astype(F32) * (dots - correction)).astype(BF16)
        dq_f[part, :] = mul(kh, slopes, 1, 0) * SCALE
        if h % 2 == 1:
            advance_if(4)
        if h % 3 == 2 and pending:
            step = pending.pop(0)
            line_recv(step - 1, (1,))
            line_send(step, (1,))
    for step in pending:
        line_recv(step - 1, (1,))
        line_send(step, (1,))
    for k in range(1, nb):
        to = lax.rem(me + k, nb)
        remote(stats, all_stats.at[me], ssend.at[k], srecv.at[k], "blk", to).start()
    all_stats[me] = stats[...]
    dq = head_norm_pull(queries, q_scaling, dq_f[...]).astype(BF16)
    terms[3] = mul(attn_t[...], gout[...], 1, 0).astype(BF16)
    begin(3)
    terms[0] = mul(normed, dq, 0, 1).astype(BF16)
    begin(0)
    out = x + mul(mean_rows[...], wm[...], 1, 0) + mul(attn_t[...], wo[...], 0, 0)
    layer[...] = out.astype(BF16)
    for k in range(1, nd):
        swap(sback, rback, bsend, brecv, k, True).wait_recv()
    halo = mul(onehot[...], rback[...].reshape(nd * cap, width), 1, 0)

    own_keys, k_scaling = head_norm(mul(wk[...], normed, 0, 1))
    k_own = own_keys.reshape(width, rows).astype(BF16)
    v_own = mul(wv[...], normed, 0, 1).astype(BF16)
    k_own_t[...] = k_own
    v_own_t[...] = v_own
    dk_f[...] = jnp.zeros_like(dk_f)
    dv_f[...] = jnp.zeros_like(dv_f)

    def backward(block):
        at = pl.ds(pl.multiple_of(block * rows, rows), rows)
        ga_b = mul(wo[...], gouts[block], 1, 1).reshape(HEADS, HEAD_DIM, rows)
        inv_b = all_stats[block, :HEADS, :]
        gh_t[...] = (ga_b * inv_b[:, None, :]).reshape(width, rows).astype(BF16)

        def one(h, part):
            qh, gh = q_t[part, at], gh_t[part, :]
            weights = jnp.exp(mul(k_own_t[part, :], qh, 0, 0) + bias_own[:, at])
            dots = mul(v_own_t[part, :], gh, 0, 0)
            correction = all_stats[block, pl.ds(HEADS + h, 1), :]
            slopes = (weights * (dots - correction)).astype(BF16)
            dk_f[part, :] += mul(qh, slopes, 1, 1)
            dv_f[part, :] += mul(gh, weights.astype(BF16), 1, 1)

        heads(one)

    backward(me)
    for p in (4, 3, 0):
        advance_if(p)
    for k in range(1, nb):
        to = lax.rem(me + k, nb)
        origin = lax.rem(me + nb - k, nb)
        remote(stats, all_stats.at[origin], ssend.at[k], srecv.at[k], "blk", to).wait()
    for distance in range(1, nb - 1):
        at_distance(distance, backward)
        for p in (4, 3, 0):
            advance_if(p)
    line_recv(nb - 2, (1,))
    at_distance(nb - 1, backward)
    for p in (4, 3, 0):
        advance_if(p)
    dk = head_norm_pull(own_keys, k_scaling, dk_f[...]).astype(BF16)
    dv = dv_f[...].astype(BF16)
    terms[2] = mul(normed, dv, 0, 1).astype(BF16)
    begin(2)
    terms[1] = mul(normed, dk, 0, 1).astype(BF16)
    begin(1)
    for p in (4, 3, 0):
        advance_if(p)
    dnormed = (mul(wq[...], dq, 1, 0) + mul(wk[...], dk, 1, 0) + mul(wv[...], dv, 1, 0)).T
    dnormed = dnormed + halo
    xs = x * scaling
    gacc[0] = jnp.broadcast_to(jnp.sum(dnormed * xs, axis=0, keepdims=True), gacc.shape[1:])
    gain_copy(0).start()
    dscaled = dnormed * gain[...]
    dx = scaling * (dscaled - xs * jnp.mean(dscaled * xs, axis=-1, keepdims=True))
    fgrad[...] = (gout[...].astype(F32) + dx).astype(BF16)
    turn = 0
    while any(stage[p] < stages for p in range(PIECES)) or turn <= n:
        for p in (2, 1, 3, 0, 4):
            advance_if(p)
        gain_turn(turn)
        turn += 1

    for p in range(PIECES):
        settle(p)
    for step in range(nb - 1):
        line_send(step, (0, 1, 2), False)
    for k in range(1, nd):
        swap(sbuf, rbuf, asend, arecv, k, False).wait_send()
        swap(sback, rback, bsend, brecv, k, False).wait_send()


def layer_call(nd, nb, *args):
    feat, sidx = args[0], args[9]
    rows, width = feat.shape
    cap = sidx.shape[1]
    total, slots = nb * rows, nd * cap
    vmem = pl.BlockSpec(memory_space=pltpu.VMEM)
    smem = pl.BlockSpec(memory_space=pltpu.SMEM)
    dma = pltpu.SemaphoreType.DMA
    V = pltpu.VMEM
    n = len(plan(nd, width, False))
    last = plan(nd, width, False)[-1][1]
    lines = [V((nb, line_rows(nb, last), width), BF16)] * PIECES
    buffers = []
    for flip in FLIPS:
        for _, count, _ in plan(nd, width, flip):
            buffers += [V((count, width), BF16)] * 2
    return pl.pallas_call(
        partial(layer_kernel, nd, nb),
        out_shape=[
            jax.ShapeDtypeStruct((rows, width), BF16),
            jax.ShapeDtypeStruct((rows, width), BF16),
            jax.ShapeDtypeStruct((PIECES * width, width), BF16),
            jax.ShapeDtypeStruct((1, width), F32),
        ],
        in_specs=[vmem] * 12 + [smem] * 2,
        out_specs=[vmem] * 4,
        scratch_shapes=[
            V((nb, rows, width), BF16), V((nb, rows, width), BF16),
            V((nb, 16, rows), jnp.int32), V((16, rows), jnp.int32),
            V((nd, cap, width), BF16), V((nd, cap, width), BF16),
            V((nd, cap, width), BF16), V((nd, cap, width), BF16),
            V((rows, slots), F32), V((rows, slots), BF16),
            V((width, total), BF16), V((width, total), BF16), V((width, total), BF16),
            V((width, rows), BF16), V((width, rows), F32), V((width, rows), BF16),
            V((rows, width), BF16),
            V((rows, rows), F32), V((rows, total), F32),
            V((width, rows), F32), V((width, rows), F32), V((width, rows), F32),
            V((width, rows), BF16), V((width, rows), BF16), V((width, rows), BF16),
            V((2 * HEADS, rows), F32), V((nb, 2 * HEADS, rows), F32),
            V((PIECES, width, width), BF16),
            V((n + 1, 8, width), F32), V((n, 8, width), F32),
            dma((2, nb, 3)), dma((2, nb, 3)),
            dma((nd,)), dma((nd,)), dma((nd,)), dma((nd,)), dma((nb,)), dma((nb,)),
            dma((PIECES, n)), dma((PIECES, n)), dma((n,)), dma((n,)),
            dma((PIECES, n)), dma((PIECES, n)),
            dma((PIECES, nb)), dma((PIECES, nb)), dma((PIECES, nb)), dma((PIECES, nb)),
            dma((nb,)), dma((nb,)),
            V((nb, 8, width), F32),
            V((HEADS, total, rows), BF16), V((width, rows), F32), V((HEADS, rows), F32),
        ]
        + buffers
        + lines,
        compiler_params=params(0),
    )(*args)


def widen_kernel(x, out):
    out[0] = x[...].astype(F32)


def widen(sums):
    width = sums.shape[1]
    return pl.pallas_call(
        widen_kernel,
        grid=(PIECES,),
        out_shape=jax.ShapeDtypeStruct((PIECES, width, width), F32),
        in_specs=[pl.BlockSpec((width, width), lambda i: (i, 0))],
        out_specs=pl.BlockSpec((1, width, width), lambda i: (i, 0, 0)),
        compiler_params=params(),
    )(sums)


def local(
    node_features, norm_gain, w_query, w_key, w_value, w_out, w_message, node_cluster,
    block_pattern, send_rows, send_counts, edge_src, edge_dst, out_grad,
):
    rows, width = node_features.shape
    nd = lax.axis_size("dom")
    nb = lax.axis_size("blk")
    layer_out, feature_grad, sums, gain_sum = layer_call(
        nd, nb, node_features, out_grad, norm_gain.reshape(1, width),
        w_query, w_key, w_value, w_out, w_message, node_cluster.reshape(1, rows), send_rows,
        edge_src.reshape(1, -1), edge_dst.reshape(1, -1), send_counts, block_pattern,
    )
    return (layer_out, feature_grad, widen(sums), gain_sum.reshape(width))


def solution(mesh):
    nodes = P(("dom", "blk"))
    wide = P(("dom", "blk"), None)
    placed = (
        wide, P(), P(), P(), P(), P(), P(), nodes, wide, wide, nodes, nodes, nodes, wide,
    )
    return jax.shard_map(
        local,
        mesh=mesh,
        in_specs=placed,
        out_specs=(wide, wide, P(), P()),
        check_vma=False,
    )
```

```python
from functools import partial

import jax
import jax.numpy as jnp
from jax import lax
from jax.experimental import pallas as pl
from jax.experimental.pallas import tpu as pltpu
from jax.sharding import PartitionSpec as P

HEADS = 8
HEAD_DIM = 64
SCALE = 8.0 / HEAD_DIM
SHIFT = 8.0
EPS = 1e-06
MASKED = -1e30
EDGE_PART = 512
MESH = pl.DeviceIdType.MESH
F32 = jnp.float32
BF16 = jnp.bfloat16


def params(collective_id=None):
    return pltpu.CompilerParams(
        vmem_limit_bytes=56 * 1024 * 1024,
        collective_id=collective_id,
        has_side_effects=collective_id is not None,
    )


def mul(a, b, ca, cb):
    return lax.dot_general(a, b, (((ca,), (cb,)), ((), ())), preferred_element_type=F32)


def row_scale(x):
    return lax.rsqrt(jnp.mean(x * x, axis=-1, keepdims=True) + EPS)


def head_norm(x):
    view = x.reshape(HEADS, HEAD_DIM, x.shape[1])
    scaling = lax.rsqrt(jnp.mean(view * view, axis=1, keepdims=True) + EPS)
    return view * scaling, scaling


def head_norm_pull(y, scaling, dy):
    dy = dy.reshape(y.shape)
    dx = scaling * (dy - y * jnp.mean(y * dy, axis=1, keepdims=True))
    return dx.reshape(-1, y.shape[2])


def remote(src, dst, send, recv, axis, peer):
    return pltpu.make_async_remote_copy(
        src_ref=src, dst_ref=dst, send_sem=send, recv_sem=recv,
        device_id={axis: peer}, device_id_type=MESH,
    )


def plan(nd, rows, flip):
    bits = [1 << i for i in range(nd.bit_length() - 1)]
    if flip:
        bits = bits[:1] + bits[:0:-1]
    steps = []
    for bit in bits:
        halves = rows % 32 == 0
        rows = rows // 2 if halves else rows
        steps.append((bit, rows, halves))
    return steps


def line_rows(nb, rows):
    return rows // nb if rows % (16 * nb) == 0 else rows


FLIPS = (True, False, True, False, True)
PIECES = len(FLIPS)


def layer_kernel(
    nd, nb,
    feat, gout, gain, wq, wk, wv, wo, wm, labels, sidx, esrc, edst, live_counts, pattern,
    layer, fgrad, sums, gsum,
    feats, gouts, metas, mine, sbuf, rbuf, sback, rback, cnt, onehot,
    k_t, v_t, q_t, q_own, ga_t, attn_t, mean_rows, bias, bias_own, dq_f, dk_f, dv_f, gh_t, k_own_t, v_own_t,
    stats, all_stats, terms, gacc, grecv,
    zsend, zrecv, asend, arecv, bsend, brecv, ssend, srecv,
    rsend, rrecv, gsend, grsem, hsend, hrecv, lsend, lrecv, tsend, trecv, usend, urecv, gline,
    w_all, num, den,
    *buffers,
):
    me = lax.axis_index("blk")
    my_dom = lax.axis_index("dom")
    index = {"dom": my_dom, "blk": me}
    rows, width = feat.shape
    cap = sidx.shape[1]
    plans = [plan(nd, width, f) for f in FLIPS]
    n = len(plans[0])
    acc = [[buffers[2 * (p * n + s)] for s in range(n)] for p in range(PIECES)]
    last = plans[0][-1][1]
    share = line_rows(nb, last)
    stages = 2 * n + 2 if share < last else 2 * n + 1
    gline_in = buffers[-PIECES:]
    got = [[buffers[2 * (p * n + s) + 1] for s in range(n)] for p in range(PIECES)]

    barrier = pltpu.get_barrier_semaphore()
    for axis, size in (("dom", nd), ("blk", nb)):
        for k in range(1, size):
            pl.semaphore_signal(
                barrier, inc=1, device_id={axis: lax.rem(index[axis] + k, size)},
                device_id_type=MESH,
            )

    own_labels = labels[...]
    mine[...] = jnp.zeros_like(mine)
    mine[0:1, :] = own_labels
    for b in range(nb):
        mine[1 + b : 2 + b, :] = jnp.where(pattern[0, b] == 1, own_labels, -1)
    pl.semaphore_wait(barrier, nd - 1 + nb - 1)

    streams = ((feat, feats), (gout, gouts), (mine, metas))

    def line_copy(step, way, k, block):
        src, dst = streams[k]
        if step > 0:
            src = dst.at[block]
        peer = me + 1 if way == 0 else me - 1
        return remote(
            src, dst.at[block], zsend.at[way, step, k], zrecv.at[way, step, k], "blk", peer
        )

    def line_send(step, kinds, start=True):
        for way in range(2):
            sends = (me + 1 < nb) & (me - step >= 0) if way == 0 else (me >= 1) & (me + step < nb)
            block = me - step if way == 0 else me + step

            @pl.when(sends)
            def _():
                for k in kinds:
                    c = line_copy(step, way, k, block)
                    if start:
                        c.start()
                    else:
                        c.wait_send()

    def line_recv(step, kinds):
        for way in range(2):
            block = me - 1 - step if way == 0 else me + 1 + step
            comes = block >= 0 if way == 0 else block < nb

            @pl.when(comes)
            def _():
                for k in kinds:
                    line_copy(step, way, k, block).wait_recv()

    def swap(src, dst, send, recv, k, incoming):
        to = lax.rem(my_dom + k, nd)
        origin = lax.rem(my_dom + nd - k, nd)
        return remote(
            src.at[to], dst.at[origin if incoming else my_dom], send.at[k], recv.at[k], "dom", to
        )

    stage = [-1] * PIECES
    first = [None] * PIECES
    history = [[] for _ in range(PIECES)]

    def aligned(start, count):
        return pl.ds(pl.multiple_of(start, 16), count)

    def peer_of(axis, bit):
        mine_bit = lax.rem(index[axis] // bit, 2)
        return mine_bit, index[axis] + bit - 2 * bit * mine_bit

    def gain_copy(s):
        bit, _, _ = plans[1][s]
        return remote(
            gacc.at[s], grecv.at[s], gsend.at[s], grsem.at[s], "dom", peer_of("dom", bit)[1]
        )

    def gain_line(k, incoming):
        to = lax.rem(me + k, nb)
        origin = lax.rem(me + nb - k, nb)
        return remote(
            gacc.at[n], gline.at[origin if incoming else me], usend.at[k], urecv.at[k], "blk", to
        )

    def gain_turn(turn):
        if turn < n:
            gain_copy(turn).wait()
            gacc[turn + 1] = gacc[turn] + grecv[turn]
            if turn + 1 < n:
                gain_copy(turn + 1).start()
            else:
                for k in range(1, nb):
                    gain_line(k, False).start()
                gline[me] = gacc[n]
        elif turn == n:
            for k in range(1, nb):
                gain_line(k, True).wait()
            total = gline[0]
            for b in range(1, nb):
                total = total + gline[b]
            gsum[...] = total[0:1, :]

    def reduce_copy(p, s):
        bit, count, halves = plans[p][s]
        bit_set, peer = peer_of("dom", bit)
        src = terms.at[p] if s == 0 else acc[p][s - 1]
        away = (1 - bit_set) * count if halves else 0
        keep = bit_set * count if halves else 0
        c = remote(
            src.at[aligned(away, count), :], got[p][s], rsend.at[p, s], rrecv.at[p, s], "dom", peer
        )
        return c, src, keep

    def share_of(b):
        return aligned(b * share, share) if share < last else aligned(0, last)

    def line_reduce(p, k, incoming):
        to = lax.rem(me + k, nb)
        origin = lax.rem(me + nb - k, nb)
        return remote(
            acc[p][n - 1].at[share_of(to), :],
            gline_in[p].at[origin if incoming else me],
            lsend.at[p, k], lrecv.at[p, k], "blk", to,
        )

    def line_spread(p, k, incoming):
        to = lax.rem(me + k, nb)
        origin = lax.rem(me + nb - k, nb)
        src = sums.at[aligned(p * width + first[p] + me * share, share), :]
        dst = sums.at[aligned(p * width + first[p] + (origin if incoming else me) * share, share), :]
        return remote(src, dst, tsend.at[p, k], trecv.at[p, k], "blk", to)

    def spread_copy(p, s):
        peer, start, count = history[p][s]
        place = sums.at[aligned(p * width + start, count), :]
        return remote(place, place, hsend.at[p, s], hrecv.at[p, s], "dom", peer)

    def back_step(p, stage_now):
        return stages - 1 - stage_now

    def launch(p):
        s = stage[p]
        if s < n:
            reduce_copy(p, s)[0].start()
        elif s == n:
            for k in range(1, nb):
                line_reduce(p, k, False).start()
            gline_in[p][me] = acc[p][n - 1][share_of(me), :]
        elif s < stages - n:
            for k in range(1, nb):
                line_spread(p, k, False).start()
        elif s < stages:
            spread_copy(p, back_step(p, s)).start()

    def begin(p):
        stage[p] = 0
        first[p] = 0
        launch(p)

    def advance(p):
        s = stage[p]
        if s < n:
            c, src, keep = reduce_copy(p, s)
            bit, count, halves = plans[p][s]
            c.wait_recv()
            total = src[aligned(keep, count), :].astype(F32) + got[p][s][...].astype(F32)
            first[p] = first[p] + keep
            history[p].append((peer_of("dom", bit)[1], first[p], count))
            acc[p][s][...] = total.astype(BF16)
        elif s == n:
            for k in range(1, nb):
                line_reduce(p, k, True).wait_recv()
            total = gline_in[p][0].astype(F32)
            for b in range(1, nb):
                total = total + gline_in[p][b].astype(F32)
            mine_at = me * share if share < last else 0
            sums[aligned(p * width + first[p] + mine_at, share), :] = total.astype(BF16)
        elif s < stages - n:
            for k in range(1, nb):
                line_spread(p, k, True).wait_recv()
        else:
            spread_copy(p, back_step(p, s)).wait_recv()
        s += 1
        while stages - n <= s < stages and not plans[p][back_step(p, s)][2]:
            s += 1
        stage[p] = s
        launch(p)

    def advance_if(p):
        if 0 <= stage[p] < stages:
            advance(p)

    def settle(p):
        for s in range(n):
            reduce_copy(p, s)[0].wait_send()
            if plans[p][s][2]:
                spread_copy(p, s).wait_send()
        for k in range(1, nb):
            line_reduce(p, k, False).wait_send()
            if share < last:
                line_spread(p, k, False).wait_send()

    line_send(0, (0, 2))
    feats[me] = feat[...]
    gouts[me] = gout[...]
    metas[me] = mine[...]

    x = feat[...].astype(F32)
    scaling = row_scale(x)
    normed = (x * scaling * gain[...]).astype(BF16)
    row_ids = lax.broadcasted_iota(jnp.int32, (rows, cap), 0)
    lane_ids = lax.broadcasted_iota(jnp.int32, (1, cap), 1)
    for p in range(nd):
        picks = jnp.where(lane_ids < live_counts[p], sidx[p : p + 1, :], -1)
        hot = jnp.where(row_ids == picks, 1.0, 0.0).astype(BF16)
        onehot[:, p * cap : (p + 1) * cap] = hot
        sbuf[p] = mul(hot, normed, 0, 0).astype(BF16)
    for k in range(1, nd):
        swap(sbuf, rbuf, asend, arecv, k, False).start()
    rbuf[my_dom] = sbuf[my_dom]

    slot_ids = lax.broadcasted_iota(jnp.int32, (nd * cap, EDGE_PART), 0)
    dst_ids = lax.broadcasted_iota(jnp.int32, (rows, EDGE_PART), 0)
    cnt[...] = jnp.zeros_like(cnt)

    def count_edges(c, carry):
        at = pl.ds(pl.multiple_of(c * EDGE_PART, EDGE_PART), EDGE_PART)
        hot_src = jnp.where(slot_ids == esrc[:, at], 1.0, 0.0).astype(BF16)
        hot_dst = jnp.where(dst_ids == edst[:, at], 1.0, 0.0).astype(BF16)
        cnt[...] += mul(hot_dst, hot_src, 1, 1)
        return carry

    lax.fori_loop(0, esrc.shape[1] // EDGE_PART, count_edges, 0)
    counts = cnt[...]
    degree = jnp.maximum(jnp.sum(counts, axis=1, keepdims=True), 1.0)
    counts = counts.astype(BF16)
    if nb > 2:
        line_recv(0, (0, 2))
        line_send(1, (0, 2))
    dmessage = (mul(gout[...], wm[...], 1, 1) / degree).astype(BF16)
    for p in range(nd):
        sback[p] = mul(counts[:, p * cap : (p + 1) * cap], dmessage, 0, 0).astype(BF16)
    for k in range(1, nd):
        swap(sback, rback, bsend, brecv, k, False).start()
    rback[my_dom] = sback[my_dom]

    own_row = own_labels.astype(F32)
    own_column = jnp.broadcast_to(own_row, (rows, rows)).T
    queries, q_scaling = head_norm(mul(wq[...], normed, 0, 1))
    q_own[...] = (queries * SCALE).reshape(q_own.shape).astype(BF16)
    ga_t[...] = mul(wo[...], gout[...], 1, 1)
    num[...] = jnp.zeros_like(num)
    den[...] = jnp.zeros_like(den)

    def heads(body):
        def pair(i, carry):
            for j in range(2):
                h = 2 * i + j
                body(h, pl.ds(pl.multiple_of(h * HEAD_DIM, HEAD_DIM), HEAD_DIM))
            return carry

        lax.fori_loop(0, HEADS // 2, pair, 0)

    def forward(block):
        at = pl.ds(pl.multiple_of(block * rows, rows), rows)
        xb = feats[block].astype(F32)
        nb_rows = (xb * row_scale(xb) * gain[...]).astype(BF16)
        keys, _ = head_norm(mul(wk[...], nb_rows, 0, 1))
        k_t[:, at] = keys.reshape(width, rows).astype(BF16)
        v_t[:, at] = mul(wv[...], nb_rows, 0, 1).astype(BF16)
        block_queries, _ = head_norm(mul(wq[...], nb_rows, 0, 1))
        q_t[:, at] = (block_queries * SCALE).reshape(width, rows).astype(BF16)
        column = jnp.broadcast_to(metas[block, 0:1, :].astype(F32), (rows, rows)).T
        seen = jnp.where(pattern[0, block] == 1, own_row, -1.0)
        bias[...] = jnp.where(column == seen, -SHIFT, MASKED)
        towards = metas[block, pl.ds(1 + me, 1), :].astype(F32)
        bias_own[:, at] = jnp.where(own_column == towards, -SHIFT, MASKED)

        def one(h, part):
            weights = jnp.exp(mul(k_t[part, at], q_own[part, :], 0, 0) + bias[...])
            den[pl.ds(h, 1), :] += jnp.sum(weights, axis=0, keepdims=True)
            weights = weights.astype(BF16)
            w_all[h, at, :] = weights
            num[part, :] += mul(v_t[part, at], weights, 1, 0)

        heads(one)

    def at_distance(distance, body):
        for way in range(2):
            block = me - distance if way == 0 else me + distance

            @pl.when(block >= 0 if way == 0 else block < nb)
            def _():
                body(block)

    forward(me)
    for k in range(1, nd):
        swap(sbuf, rbuf, asend, arecv, k, True).wait_recv()
    mean = (mul(counts, rbuf[...].reshape(nd * cap, width), 1, 0) / degree).astype(BF16)
    mean_rows[...] = mean
    terms[4] = mul(mean, gout[...], 0, 0).astype(BF16)
    begin(4)
    for step in range(2, nb - 1):
        line_recv(step - 1, (0, 2))
        line_send(step, (0, 2))
        at_distance(step - 1, forward)
        advance_if(4)
    line_recv(nb - 2, (0, 2))
    line_send(0, (1,))
    for distance in range(max(nb - 2, 1), nb):
        at_distance(distance, forward)
        advance_if(4)

    inv = 1.0 / den[...]
    ga_heads = ga_t[...].reshape(HEADS, HEAD_DIM, rows)
    attn = (num[...].reshape(HEADS, HEAD_DIM, rows) * inv[:, None, :]).astype(BF16)
    correction = jnp.sum(ga_heads * attn.astype(F32), axis=1) * inv
    attn_t[...] = attn.reshape(width, rows)
    gh_t[...] = (ga_heads * inv[:, None, :]).reshape(width, rows).astype(BF16)
    stats[:HEADS, :] = inv
    stats[HEADS:, :] = correction
    for k in range(1, nb):
        to = lax.rem(me + k, nb)
        remote(stats, all_stats.at[me], ssend.at[k], srecv.at[k], "blk", to).start()
    all_stats[me] = stats[...]
    terms[3] = mul(attn_t[...], gout[...], 1, 0).astype(BF16)
    begin(3)

    for h in range(HEADS):
        part = slice(h * HEAD_DIM, (h + 1) * HEAD_DIM)
        dots = mul(v_t[part, :], gh_t[part, :], 0, 0)
        slopes = (w_all[h].astype(F32) * (dots - stats[HEADS + h : HEADS + h + 1, :])).astype(BF16)
        dq_f[part, :] = mul(k_t[part, :], slopes, 1, 0) * SCALE
        if h == 5:
            for step in range(1, min(2, nb - 1)):
                line_recv(step - 1, (1,))
                line_send(step, (1,))
        if h % 4 == 3:
            advance_if(4)
            advance_if(3)
    dq = head_norm_pull(queries, q_scaling, dq_f[...]).astype(BF16)
    terms[0] = mul(normed, dq, 0, 1).astype(BF16)
    begin(0)
    out = x + mul(mean_rows[...], wm[...], 1, 0) + mul(attn_t[...], wo[...], 0, 0)
    layer[...] = out.astype(BF16)
    for k in range(1, nd):
        swap(sback, rback, bsend, brecv, k, True).wait_recv()
    halo = mul(onehot[...], rback[...].reshape(nd * cap, width), 1, 0)

    own_keys, k_scaling = head_norm(mul(wk[...], normed, 0, 1))
    k_own = own_keys.reshape(width, rows).astype(BF16)
    v_own = mul(wv[...], normed, 0, 1).astype(BF16)
    k_own_t[...] = k_own
    v_own_t[...] = v_own
    dk_f[...] = jnp.zeros_like(dk_f)
    dv_f[...] = jnp.zeros_like(dv_f)

    def backward(block):
        at = pl.ds(pl.multiple_of(block * rows, rows), rows)
        ga_b = mul(wo[...], gouts[block], 1, 1).reshape(HEADS, HEAD_DIM, rows)
        inv_b = all_stats[block, :HEADS, :]
        gh_t[...] = (ga_b * inv_b[:, None, :]).reshape(width, rows).astype(BF16)

        def one(h, part):
            qh, gh = q_t[part, at], gh_t[part, :]
            weights = jnp.exp(mul(k_own_t[part, :], qh, 0, 0) + bias_own[:, at])
            dots = mul(v_own_t[part, :], gh, 0, 0)
            correction = all_stats[block, pl.ds(HEADS + h, 1), :]
            slopes = (weights * (dots - correction)).astype(BF16)
            dk_f[part, :] += mul(qh, slopes, 1, 1)
            dv_f[part, :] += mul(gh, weights.astype(BF16), 1, 1)

        heads(one)

    backward(me)
    for p in (4, 3, 0):
        advance_if(p)
    for k in range(1, nb):
        to = lax.rem(me + k, nb)
        origin = lax.rem(me + nb - k, nb)
        remote(stats, all_stats.at[origin], ssend.at[k], srecv.at[k], "blk", to).wait()
    for distance in range(1, nb - 1):
        if distance > 1:
            line_recv(distance - 1, (1,))
            line_send(distance, (1,))
        at_distance(distance, backward)
        for p in (4, 3, 0):
            advance_if(p)
    line_recv(nb - 2, (1,))
    at_distance(nb - 1, backward)
    for p in (4, 3, 0):
        advance_if(p)
    dk = head_norm_pull(own_keys, k_scaling, dk_f[...]).astype(BF16)
    dv = dv_f[...].astype(BF16)
    terms[2] = mul(normed, dv, 0, 1).astype(BF16)
    begin(2)
    terms[1] = mul(normed, dk, 0, 1).astype(BF16)
    begin(1)
    for p in (4, 3, 0):
        advance_if(p)
    dnormed = (mul(wq[...], dq, 1, 0) + mul(wk[...], dk, 1, 0) + mul(wv[...], dv, 1, 0)).T
    dnormed = dnormed + halo
    xs = x * scaling
    gacc[0] = jnp.broadcast_to(jnp.sum(dnormed * xs, axis=0, keepdims=True), gacc.shape[1:])
    gain_copy(0).start()
    dscaled = dnormed * gain[...]
    dx = scaling * (dscaled - xs * jnp.mean(dscaled * xs, axis=-1, keepdims=True))
    fgrad[...] = (gout[...].astype(F32) + dx).astype(BF16)
    turn = 0
    while any(stage[p] < stages for p in range(PIECES)) or turn <= n:
        for p in (2, 1, 3, 0, 4):
            advance_if(p)
        gain_turn(turn)
        turn += 1

    for p in range(PIECES):
        settle(p)
    for step in range(nb - 1):
        line_send(step, (0, 1, 2), False)
    for k in range(1, nd):
        swap(sbuf, rbuf, asend, arecv, k, False).wait_send()
        swap(sback, rback, bsend, brecv, k, False).wait_send()


def layer_call(nd, nb, *args):
    feat, sidx = args[0], args[9]
    rows, width = feat.shape
    cap = sidx.shape[1]
    total, slots = nb * rows, nd * cap
    vmem = pl.BlockSpec(memory_space=pltpu.VMEM)
    smem = pl.BlockSpec(memory_space=pltpu.SMEM)
    dma = pltpu.SemaphoreType.DMA
    V = pltpu.VMEM
    n = len(plan(nd, width, False))
    last = plan(nd, width, False)[-1][1]
    lines = [V((nb, line_rows(nb, last), width), BF16)] * PIECES
    buffers = []
    for flip in FLIPS:
        for _, count, _ in plan(nd, width, flip):
            buffers += [V((count, width), BF16)] * 2
    return pl.pallas_call(
        partial(layer_kernel, nd, nb),
        out_shape=[
            jax.ShapeDtypeStruct((rows, width), BF16),
            jax.ShapeDtypeStruct((rows, width), BF16),
            jax.ShapeDtypeStruct((PIECES * width, width), BF16),
            jax.ShapeDtypeStruct((1, width), F32),
        ],
        in_specs=[vmem] * 12 + [smem] * 2,
        out_specs=[vmem] * 4,
        scratch_shapes=[
            V((nb, rows, width), BF16), V((nb, rows, width), BF16),
            V((nb, 16, rows), jnp.int32), V((16, rows), jnp.int32),
            V((nd, cap, width), BF16), V((nd, cap, width), BF16),
            V((nd, cap, width), BF16), V((nd, cap, width), BF16),
            V((rows, slots), F32), V((rows, slots), BF16),
            V((width, total), BF16), V((width, total), BF16), V((width, total), BF16),
            V((width, rows), BF16), V((width, rows), F32), V((width, rows), BF16),
            V((rows, width), BF16),
            V((rows, rows), F32), V((rows, total), F32),
            V((width, rows), F32), V((width, rows), F32), V((width, rows), F32),
            V((width, rows), BF16), V((width, rows), BF16), V((width, rows), BF16),
            V((2 * HEADS, rows), F32), V((nb, 2 * HEADS, rows), F32),
            V((PIECES, width, width), BF16),
            V((n + 1, 8, width), F32), V((n, 8, width), F32),
            dma((2, nb, 3)), dma((2, nb, 3)),
            dma((nd,)), dma((nd,)), dma((nd,)), dma((nd,)), dma((nb,)), dma((nb,)),
            dma((PIECES, n)), dma((PIECES, n)), dma((n,)), dma((n,)),
            dma((PIECES, n)), dma((PIECES, n)),
            dma((PIECES, nb)), dma((PIECES, nb)), dma((PIECES, nb)), dma((PIECES, nb)),
            dma((nb,)), dma((nb,)),
            V((nb, 8, width), F32),
            V((HEADS, total, rows), BF16), V((width, rows), F32), V((HEADS, rows), F32),
        ]
        + buffers
        + lines,
        compiler_params=params(0),
    )(*args)


def widen_kernel(x, out):
    out[0] = x[...].astype(F32)


def widen(sums):
    width = sums.shape[1]
    return pl.pallas_call(
        widen_kernel,
        grid=(PIECES,),
        out_shape=jax.ShapeDtypeStruct((PIECES, width, width), F32),
        in_specs=[pl.BlockSpec((width, width), lambda i: (i, 0))],
        out_specs=pl.BlockSpec((1, width, width), lambda i: (i, 0, 0)),
        compiler_params=params(),
    )(sums)


def local(
    node_features, norm_gain, w_query, w_key, w_value, w_out, w_message, node_cluster,
    block_pattern, send_rows, send_counts, edge_src, edge_dst, out_grad,
):
    rows, width = node_features.shape
    nd = lax.axis_size("dom")
    nb = lax.axis_size("blk")
    layer_out, feature_grad, sums, gain_sum = layer_call(
        nd, nb, node_features, out_grad, norm_gain.reshape(1, width),
        w_query, w_key, w_value, w_out, w_message, node_cluster.reshape(1, rows), send_rows,
        edge_src.reshape(1, -1), edge_dst.reshape(1, -1), send_counts, block_pattern,
    )
    return (layer_out, feature_grad, widen(sums), gain_sum.reshape(width))


def solution(mesh):
    nodes = P(("dom", "blk"))
    wide = P(("dom", "blk"), None)
    placed = (
        wide, P(), P(), P(), P(), P(), P(), nodes, wide, wide, nodes, nodes, nodes, wide,
    )
    return jax.shard_map(
        local,
        mesh=mesh,
        in_specs=placed,
        out_specs=(wide, wide, P(), P()),
        check_vma=False,
    )
```
